512 devices in a mesh: row: 16 (over y, x_lo, core), col: 32 (over x_hi, z).
Axes of the slice: x: 4 (x_hi: 2, x_lo: 2; x = x_hi * 2 + x_lo), y: 4, z: 16, core: 2. Of those that a mesh axis runs over, the one named last changes fastest.
Arguments:
- left_panel: bfloat16 [16384, 16384], P('row', 'col'), may hold values from -0.125 to 0.125
- right_panel: bfloat16 [16384, 16384], P('row', 'col'), may hold values from -6 to 6
- earlier_terms: bfloat16 [16384, 16384], P('row', 'col'), may hold values from 0 to 1
- density: bfloat16 [16384, 16384], P('row', 'col'), may hold values from -3 to 3
- left_occupied: int32 [32, 32], P('row', 'col'), may hold values from 0 to 1, as said below
- right_occupied: int32 [32, 32], P('row', 'col'), may hold values from 0 to 1, as said below
- kept_tiles: int32 [32, 32], P('row', 'col'), may hold values from 0 to 1, as said below
- branch: int32 [32], P('row'), may hold values from 0 to 1, as said below
Outputs:
- new_density: bfloat16 [16384, 16384], P('row', 'col')
- occupation: float32 [1], replicated
The draws below stay inside these ranges and needn't reach their ends.
Inputs may be any that keep to these rules, and one draw needn't show every extreme that they name: `left_occupied`: 1 marks an occupied tile, 0 an empty one; of the 2 x 1 tiles of one device's block at most 1 are occupied, and some device's block holds exactly 1. `right_occupied`: 1 marks an occupied tile, 0 an empty one; of the 2 x 1 tiles of one device's block at most 1 are occupied, and some device's block holds exactly 1. `kept_tiles`: 1 marks a tile kept in the new matrix. `branch`: for each tile row, 1 selects X squared, 0 selects 2 X minus X squared; both values occur.
All inputs are finite; a program needn't handle non-finite values.
Results may differ from the reference program's by a relative error of at most 0.001.
Values may be sent and summed in bfloat16 or wider, within the bound.
No kernel may reach another device: no remote copies, remote signals or barrier semaphores. Data moves between devices by JAX's collectives and lax.ppermute only.
A program may use at most 64 MiB of HBM per device.

```python
import jax
import jax.numpy as jnp
from jax import lax

TILE = 512
CT = 1
STEPS = 4
BLK_COLS = 512
BLK_ROWS = 1024
NPANEL = 32
ORDER = 16384
NTILES = 32


def block_occupancy(key):
    row_blocks = NTILES // (2 * CT)
    col_blocks = NTILES // CT
    per_block = 2 * CT * CT
    capacity = CT * CT
    score_key, filled_key, part_key, force_key = jax.random.split(key, 4)
    scores = jax.random.randint(score_key, (row_blocks, col_blocks, per_block), 0, 1 << 20, dtype=jnp.int32)
    scores = scores * per_block + jnp.arange(per_block, dtype=jnp.int32)
    ranking = jnp.argsort(jnp.argsort(scores, axis=-1), axis=-1).astype(jnp.int32)
    filled = jax.random.randint(filled_key, (row_blocks, col_blocks), 0, 5, dtype=jnp.int32) < 4
    partial_value = jax.random.randint(part_key, (row_blocks, col_blocks), 0, capacity, dtype=jnp.int32)
    counts = jnp.where(filled, capacity, partial_value)
    chosen = jax.random.randint(force_key, (), 0, row_blocks * col_blocks, dtype=jnp.int32)
    flat_index = jnp.arange(row_blocks * col_blocks, dtype=jnp.int32).reshape(row_blocks, col_blocks)
    counts = jnp.where(flat_index == chosen, capacity, counts)
    occupied = (ranking < counts[:, :, None]).astype(jnp.int32)
    occupied = occupied.reshape(row_blocks, col_blocks, 2 * CT, CT).transpose(0, 2, 1, 3)
    return occupied.reshape(NTILES, NTILES)


def draw_left_occupied(key, part):
    key = jax.random.fold_in(key, 11)
    return block_occupancy(key)


def draw_right_occupied(key, part):
    key = jax.random.fold_in(key, 23)
    return block_occupancy(key)


def draw_kept_tiles(key, part):
    key = jax.random.fold_in(key, 37)
    tile_rows = jnp.arange(NTILES, dtype=jnp.int32)[:, None]
    percent = 20 + 40 * tile_rows // max(NTILES - 1, 1)
    uniform_ints = jax.random.randint(key, (NTILES, NTILES), 0, 100, dtype=jnp.int32)
    return (uniform_ints < percent).astype(jnp.int32)


def draw_branch(key, part):
    key = jax.random.fold_in(key, 53)
    flag_key, zero_key, step_key = jax.random.split(key, 3)
    flags = jax.random.randint(flag_key, (NTILES,), 0, 2, dtype=jnp.int32)
    zero_at = jax.random.randint(zero_key, (), 0, NTILES, dtype=jnp.int32)
    one_at = (zero_at + jax.random.randint(step_key, (), 1, NTILES, dtype=jnp.int32)) % NTILES
    positions = jnp.arange(NTILES, dtype=jnp.int32)
    flags = jnp.where(positions == zero_at, 0, flags)
    flags = jnp.where(positions == one_at, 1, flags)
    return flags.astype(jnp.int32)


def block_scale(key, extent, shards, least, top_value):
    def one(dim, blocks):
        draws = jax.random.uniform(jax.random.fold_in(jax.random.fold_in(key, 6), dim), (blocks,), jnp.float32, least / len(shards), top_value / len(shards))
        return jnp.repeat(jnp.exp(draws), extent[dim] // blocks).reshape((-1,) + (1,) * (len(extent) - dim - 1))

    gain = one(*shards[0])
    for cut in shards[1:]:
        gain = gain * one(*cut)
    return gain


def normal_values(key, shape, width, limit, cuts=(), kind=jnp.bfloat16):
    loudness = block_scale(key, shape, cuts, -0.22, 0.18) if cuts else 1.0
    values = jax.random.normal(key, shape, jnp.float32) * width * loudness
    return jnp.minimum(jnp.maximum(values, -limit), limit).astype(kind)


def setup_inputs(seed: int = 0) -> dict:
    streams_of = jax.random.split(jax.random.key(seed), 9)
    return {
        "left_panel": normal_values(streams_of[0], (ORDER, ORDER), (STEPS * BLK_COLS) ** -0.5, 0.125, ((0, 16), (1, 32))),
        "right_panel": normal_values(streams_of[1], (ORDER, ORDER), 1.0, 6.0, ((0, 16), (1, 32))),
        "earlier_terms": jnp.clip(1.0 * jax.random.uniform(streams_of[2], (ORDER, ORDER), jnp.float32) ** block_scale(streams_of[2], (ORDER, ORDER), ((0, 16), (1, 32)), -0.2, 0.2), 0.0, 1.0).astype(jnp.bfloat16),
        "density": normal_values(streams_of[3], (ORDER, ORDER), 0.5, 3.0, ((0, 16), (1, 32))),
        "left_occupied": draw_left_occupied(jax.random.fold_in(streams_of[8], 71), 0),
        "right_occupied": draw_right_occupied(jax.random.fold_in(streams_of[8], 71), 0),
        "kept_tiles": draw_kept_tiles(jax.random.fold_in(streams_of[8], 71), 0),
        "branch": draw_branch(jax.random.fold_in(streams_of[8], 71), 0),
    }


def spread(occupied):
    return jnp.repeat(jnp.repeat(occupied, TILE, axis=0), TILE, axis=1)


def reference(left_panel, right_panel, earlier_terms, density, left_occupied, right_occupied, kept_tiles, branch):
    left_tiles = left_panel * spread(left_occupied).astype(jnp.bfloat16)
    right_tiles = right_panel * spread(right_occupied).astype(jnp.bfloat16)
    right_wrapped = jnp.concatenate([right_tiles, right_tiles[:2 * BLK_ROWS]], axis=0)

    def row_block(position):
        first_row = (position * BLK_ROWS).astype(jnp.int32)
        row_slab = lax.dynamic_slice_in_dim(left_tiles, first_row, BLK_ROWS, 0)
        lower_slab = lax.dynamic_slice_in_dim(right_wrapped, first_row, 2 * BLK_ROWS, 0)
        accumulated = jnp.zeros((BLK_ROWS, NPANEL, BLK_COLS), jnp.float32)
        for turn_index in range(STEPS):
            shifted = jnp.roll(row_slab, -turn_index * BLK_COLS, axis=1)
            shifted = shifted.reshape(BLK_ROWS, NPANEL, BLK_COLS).astype(jnp.float32)
            sub_panel = lower_slab[turn_index * BLK_COLS:(turn_index + 1) * BLK_COLS]
            sub_panel = sub_panel.reshape(BLK_COLS, NPANEL, BLK_COLS).astype(jnp.float32)
            accumulated = accumulated + jnp.einsum("rjk,kjl->rjl", shifted, sub_panel)
        return accumulated.reshape(BLK_ROWS, ORDER)

    product = lax.map(row_block, jnp.arange(NPANEL // 2, dtype=jnp.int32))
    product = product.reshape(ORDER, ORDER) + earlier_terms.astype(jnp.float32)
    retained = spread(kept_tiles) == 1
    row_flags = (jnp.repeat(branch, TILE) == 1)[:, None]
    chosen = jnp.where(row_flags, product, 2.0 * density.astype(jnp.float32) - product)
    combined = jnp.where(retained, chosen, jnp.zeros_like(chosen))
    occupation = (jnp.trace(combined) / ORDER).reshape(1)
    return combined.astype(jnp.bfloat16), occupation
```

```python
import jax
import jax.numpy as jnp
from jax import lax
from jax.experimental import pallas as pl
from jax.experimental.pallas import tpu as pltpu
from jax.sharding import PartitionSpec as P

FLAG_ROWS = 16
LANES = 128

VMEM = pl.BlockSpec(memory_space=pltpu.VMEM)
SMEM = pl.BlockSpec(memory_space=pltpu.SMEM)
ANY = pl.BlockSpec(memory_space=pl.ANY)


def shift(value, axis, steps):
    count = lax.axis_size(axis)
    return lax.ppermute(value, axis, [(src, (src + steps) % count) for src in range(count)])


def pack(panel, occupied):
    tile_size = panel.shape[1]
    flags = occupied[:, 0].astype(jnp.bfloat16)
    tile = lax.dynamic_slice_in_dim(panel, occupied[1, 0] * tile_size, tile_size, 0)
    lanes = lax.broadcasted_iota(jnp.int32, (FLAG_ROWS, tile_size), 1)
    tail = jnp.where(lanes < tile_size // 2, flags[0], flags[1])
    return jnp.concatenate([tile, tail], axis=0)


def flag_pair(payload):
    size = payload.shape[1]
    tail = payload[size:, :].astype(jnp.float32)
    return tail[0:1, 0:1], tail[0:1, size // 2 : size // 2 + 1]


def dot(a, b):
    return jnp.dot(a, b, preferred_element_type=jnp.float32)


def diagonal(block):
    rows = lax.broadcasted_iota(jnp.int32, block.shape, 0)
    cols = lax.broadcasted_iota(jnp.int32, block.shape, 1)
    return jnp.sum(jnp.where(rows == cols, block, 0.0), axis=(0, 1), keepdims=True)


def product_trace(left, right, size):
    total = jnp.zeros((1, 1), jnp.float32)
    for start in range(0, size, LANES):
        part = pl.ds(start, LANES)
        total = total + diagonal(dot(left(part), right[:size, part]))
    return total


def trace_kernel(
    place, right_occupied, kept, branch, own, one, chosen, right_own, right_trace, earlier, density,
    parts, earlier_tile, density_tile, sems,
):
    size = own.shape[1]
    half = lax.rem(place[1], 2)
    near_mine = lax.div(place[1], 2) == place[0]
    far_mine = lax.div(place[2], 2) == place[0]
    lanes = lax.broadcasted_iota(jnp.int32, parts.shape, 1)
    parts[...] = jnp.zeros_like(parts)

    @pl.when(near_mine)
    def _near():
        rows = pl.ds(pl.multiple_of(half * size, size), size)
        copies = [
            pltpu.make_async_copy(earlier.at[rows], earlier_tile, sems.at[0]),
            pltpu.make_async_copy(density.at[rows], density_tile, sems.at[1]),
        ]
        for copy in copies:
            copy.start()
        second = right_occupied[1, 0] == 1
        value = product_trace(lambda part: jnp.where(second, one[part, :], own[part, :]), right_own, size)
        flags = [jnp.where(second, a, b) for a, b in zip(flag_pair(one), flag_pair(own))]
        occupied = (right_occupied[0, 0] + right_occupied[1, 0]).astype(jnp.float32)
        value = value * jnp.where(half == 1, flags[1], flags[0]) * occupied
        for copy in copies:
            copy.wait()
        base = jnp.zeros((1, 1), jnp.float32)
        twice = jnp.zeros((1, 1), jnp.float32)
        for start in range(0, size, LANES):
            part = pl.ds(start, LANES)
            base = base + diagonal(earlier_tile[part, part].astype(jnp.float32))
            twice = twice + diagonal(2.0 * density_tile[part, part].astype(jnp.float32))
        squared = branch[half] == 1
        value = jnp.where(squared, base + value, twice - base - value)
        keep = (kept[half, 0] == 1).astype(jnp.float32)
        weight = jnp.where(squared, keep, -keep)
        parts[...] += jnp.where(lanes == 0, value * keep, 0.0) + jnp.where(lanes == 2, weight, 0.0)

    @pl.when(far_mine)
    def _far():
        value = product_trace(lambda part: chosen[part, :], right_trace, size)
        flags, right_flags = flag_pair(chosen), flag_pair(right_trace)
        value = value * jnp.where(half == 1, flags[1], flags[0]) * (right_flags[0] + right_flags[1])
        parts[...] += jnp.where(lanes == 1, value, 0.0)


def middle_kernel(parts, spread):
    spread[...] = jnp.broadcast_to(jnp.sum(parts[...], axis=0, keepdims=True), spread.shape)


def total_kernel(parts, total):
    values = parts[...]
    lanes = lax.broadcasted_iota(jnp.int32, values.shape, 1)
    moved = jnp.concatenate([values[-2:], values[:-2]], axis=0)
    weights = jnp.sum(jnp.where(lanes == 2, moved, 0.0), axis=1, keepdims=True)
    far = jnp.sum(jnp.where(lanes == 1, values, 0.0), axis=1, keepdims=True)
    near = jnp.sum(jnp.where(lanes == 0, values, 0.0), axis=1, keepdims=True)
    total[...] = jnp.broadcast_to(jnp.sum(near + weights * far, axis=0, keepdims=True), total.shape)


def last_kernel(
    right_occupied, kept, branch, own, one, right_own, two, right_next, earlier, density, after, out,
):
    size = own.shape[1]
    second = right_occupied[1, 0] == 1
    occupied = (right_occupied[0, 0] + right_occupied[1, 0]).astype(jnp.float32)
    first_flags = [jnp.where(second, a, b) * occupied for a, b in zip(flag_pair(one), flag_pair(own))]
    right_flags = flag_pair(right_next)
    last_flags = [flag * (right_flags[0] + right_flags[1]) for flag in flag_pair(two)]
    step = size // 4
    for start in range(0, size, step):
        part = pl.ds(start, step)
        first = dot(jnp.where(second, one[part, :], own[part, :]), right_own[:size, :])
        last = dot(two[part, :], right_next[:size, :])
        for half in range(2):
            rows = pl.ds(half * size + start, step)
            product = earlier[rows, :].astype(jnp.float32) + first_flags[half] * first + last_flags[half] * last
            other = 2.0 * density[rows, :].astype(jnp.float32) - product
            value = jnp.where(branch[half] == 1, product, other)
            value = jnp.where(kept[half, 0] == 1, value, 0.0)
            out[rows, :] = value.astype(out.dtype)


def spread_over(rows, axis):
    return lax.all_to_all(rows, axis, 0, 0, tiled=True)


def local(left_panel, right_panel, earlier, density, left_occupied, right_occupied, kept_tiles, branch):
    block_rows, size = left_panel.shape
    row_count, col_count = lax.axis_size("row"), lax.axis_size("col")
    me_row, me_col = lax.axis_index("row"), lax.axis_index("col")
    both = ("row", "col")

    left_own = pack(left_panel, left_occupied)
    left_one = shift(left_own, "col", -1)

    right_own = pack(right_panel, right_occupied)
    to_trace = [
        (((j // 2 + 1) % row_count) * col_count + j, (j // 2) * col_count + (j + 2) % col_count)
        for j in range(col_count)
    ]
    right_trace = lax.ppermute(right_own, both, to_trace)

    to_wanted = [
        (((i + 1) % row_count) * col_count + j, i * col_count + (j + 2) % col_count)
        for i in range(row_count)
        for j in range(col_count)
    ]
    wanted = lax.ppermute(jnp.broadcast_to(right_occupied[1, 0], (8, LANES)), both, to_wanted)
    right_next = shift(right_own, "row", -1)

    chosen = jnp.where(wanted[0, 0] == 1, left_one, left_own)
    left_two = shift(chosen, "col", -2)

    place = jnp.stack([me_row, me_col, (me_col + col_count - 2) % col_count])
    parts = pl.pallas_call(
        trace_kernel,
        out_shape=jax.ShapeDtypeStruct((row_count, LANES), jnp.float32),
        in_specs=[SMEM] * 4 + [VMEM] * 5 + [ANY] * 2,
        out_specs=VMEM,
        scratch_shapes=[
            pltpu.VMEM((size, size), earlier.dtype),
            pltpu.VMEM((size, size), density.dtype),
            pltpu.SemaphoreType.DMA((2,)),
        ],
        compiler_params=pltpu.CompilerParams(vmem_limit_bytes=16 * 2**20),
        name="trace",
    )(place, right_occupied, kept_tiles, branch, left_own, left_one, chosen, right_own, right_trace, earlier, density)
    parts = spread_over(parts, "row")
    parts = pl.pallas_call(
        middle_kernel,
        out_shape=jax.ShapeDtypeStruct((col_count, LANES), jnp.float32),
        in_specs=[VMEM],
        out_specs=VMEM,
        name="middle",
    )(parts)
    parts = spread_over(parts, "col")
    total = pl.pallas_call(
        total_kernel,
        out_shape=jax.ShapeDtypeStruct((8, LANES), jnp.float32),
        in_specs=[VMEM],
        out_specs=VMEM,
        name="total",
    )(parts)
    occupation = total[0, :1] / (row_count * block_rows)

    new_density = pl.pallas_call(
        last_kernel,
        out_shape=jax.ShapeDtypeStruct((block_rows, size), jnp.bfloat16),
        in_specs=[SMEM] * 3 + [VMEM] * 7 + [ANY],
        out_specs=VMEM,
        compiler_params=pltpu.CompilerParams(vmem_limit_bytes=16 * 2**20),
        name="last",
    )(right_occupied, kept_tiles, branch, left_own, left_one, right_own, left_two, right_next, earlier, density, total)
    return new_density, occupation


def solution(mesh):
    whole = P("row", "col")
    in_specs = (whole,) * 7 + (P("row"),)
    return jax.shard_map(local, mesh=mesh, in_specs=in_specs, out_specs=(whole, P()), check_vma=False)
```

```python
import functools

import jax
import jax.numpy as jnp
from jax import lax
from jax.experimental import pallas as pl
from jax.experimental.pallas import tpu as pltpu
from jax.sharding import PartitionSpec as P

FLAG_ROWS = 16
LANES = 128
LEFT_LIMIT = 62 * 2**20

VMEM = pl.BlockSpec(memory_space=pltpu.VMEM)
SMEM = pl.BlockSpec(memory_space=pltpu.SMEM)
HBM = pl.BlockSpec(memory_space=pltpu.HBM)


def call(kernel, name, ins, outs, out_specs, scratch=(), limit=12 * 2**20):
    return pl.pallas_call(
        kernel,
        out_shape=outs,
        in_specs=[spec for _, spec in ins],
        out_specs=out_specs,
        scratch_shapes=list(scratch),
        compiler_params=pltpu.CompilerParams(vmem_limit_bytes=limit),
        name=name,
    )(*[array for array, _ in ins])


def shift(value, axis, steps):
    count = lax.axis_size(axis)
    return lax.ppermute(value, axis, [(src, (src + steps) % count) for src in range(count)])


def pack_tile(occupied, panel, packed, tail, sems):
    size = panel.shape[1]
    rows = pl.ds(pl.multiple_of(occupied[1] * size, size), size)
    tile = pltpu.make_async_copy(panel.at[rows], packed.at[:size], sems.at[0])
    tile.start()
    lanes = lax.broadcasted_iota(jnp.int32, tail.shape, 1)
    flags = [occupied[k].astype(jnp.float32) for k in range(2)]
    tail[...] = jnp.where(lanes < size // 2, flags[0], flags[1]).astype(tail.dtype)
    below = pltpu.make_async_copy(tail, packed.at[size:], sems.at[1])
    below.start()
    tile.wait()
    below.wait()


def left_kernel(occupied, right_occupied, panel, packed, wanted, tail, sems):
    wanted[...] = jnp.full(wanted.shape, right_occupied[1], wanted.dtype)
    pack_tile(occupied, panel, packed, tail, sems)


def right_kernel(occupied, panel, packed, tail, sems):
    pack_tile(occupied, panel, packed, tail, sems)


def base_kernel(kept, branch, earlier, density, base, earlier_tile, density_tile, sems):
    size = earlier_tile.shape[0]
    row, col = lax.axis_index("row"), lax.axis_index("col")
    half = lax.rem(col, 2)
    base[...] = jnp.zeros_like(base)

    @pl.when(lax.div(col, 2) == row)
    def _mine():
        rows = pl.ds(pl.multiple_of(half * size, size), size)
        copies = [
            pltpu.make_async_copy(earlier.at[rows], earlier_tile, sems.at[0]),
            pltpu.make_async_copy(density.at[rows], density_tile, sems.at[1]),
        ]
        for copy in copies:
            copy.start()
        for copy in copies:
            copy.wait()
        once = jnp.zeros((1, 1), jnp.float32)
        twice = jnp.zeros((1, 1), jnp.float32)
        for start in range(0, size, LANES):
            part = pl.ds(start, LANES)
            once = once + diagonal(earlier_tile[part, part].astype(jnp.float32))
            twice = twice + diagonal(2.0 * density_tile[part, part].astype(jnp.float32))
        squared = branch[half] == 1
        keep = (kept[half] == 1).astype(jnp.float32)
        lanes = lax.broadcasted_iota(jnp.int32, base.shape, 1)
        value = keep * jnp.where(squared, once, twice - once)
        weight = jnp.where(squared, keep, -keep)
        base[...] = jnp.where(lanes == 0, value, 0.0) + jnp.where(lanes == 2, weight, 0.0)


def flag_pair(payload):
    size = payload.shape[1]
    tail = payload[size:, :].astype(jnp.float32)
    return tail[0:1, 0:1], tail[0:1, size // 2 : size // 2 + 1]


def dot(a, b):
    return jnp.dot(a, b, preferred_element_type=jnp.float32)


def diagonal(block):
    rows = lax.broadcasted_iota(jnp.int32, block.shape, 0)
    cols = lax.broadcasted_iota(jnp.int32, block.shape, 1)
    return jnp.sum(jnp.where(rows == cols, block, 0.0), axis=(0, 1), keepdims=True)


def product_trace(left, right, size):
    total = jnp.zeros((1, 1), jnp.float32)
    for start in range(0, size, LANES):
        part = pl.ds(start, LANES)
        total = total + diagonal(dot(left(part), right[:size, part]))
    return total


def trace_kernel(right_occupied, own, one, chosen, right_own, right_trace, base, parts):
    size = own.shape[1]
    row, col = lax.axis_index("row"), lax.axis_index("col")
    count = lax.axis_size("col")
    half = lax.rem(col, 2)
    lanes = lax.broadcasted_iota(jnp.int32, (1, LANES), 1)
    parts[...] = jnp.zeros_like(parts)

    @pl.when(lax.div(col, 2) == row)
    def _near():
        second = right_occupied[1] == 1
        value = product_trace(lambda part: jnp.where(second, one[part, :], own[part, :]), right_own, size)
        flags = [jnp.where(second, a, b) for a, b in zip(flag_pair(one), flag_pair(own))]
        occupied = (right_occupied[0] + right_occupied[1]).astype(jnp.float32)
        value = value * jnp.where(half == 1, flags[1], flags[0]) * occupied
        known = base[0:1, :]
        weight = jnp.sum(jnp.where(lanes == 2, known, 0.0), axis=1, keepdims=True)
        parts[...] += known + jnp.where(lanes == 0, value * weight, 0.0)

    @pl.when(lax.div(lax.rem(col + count - 2, count), 2) == row)
    def _far():
        value = product_trace(lambda part: chosen[part, :], right_trace, size)
        flags, right_flags = flag_pair(chosen), flag_pair(right_trace)
        value = value * jnp.where(half == 1, flags[1], flags[0]) * (right_flags[0] + right_flags[1])
        parts[...] += jnp.where(lanes == 1, value, 0.0)


def middle_kernel(parts, spread):
    spread[...] = jnp.broadcast_to(jnp.sum(parts[...], axis=0, keepdims=True), spread.shape)


def total_kernel(order, parts, occupation):
    values = parts[...]
    lanes = lax.broadcasted_iota(jnp.int32, values.shape, 1)
    moved = jnp.concatenate([values[-2:], values[:-2]], axis=0)
    weights = jnp.sum(jnp.where(lanes == 2, moved, 0.0), axis=1, keepdims=True)
    far = jnp.sum(jnp.where(lanes == 1, values, 0.0), axis=1, keepdims=True)
    near = jnp.sum(jnp.where(lanes == 0, values, 0.0), axis=1, keepdims=True)
    occupation[0] = jnp.sum(near + weights * far) / order


def last_kernel(
    right_occupied, kept, branch, own, one, right_own, two, right_next, earlier, density, out,
    earlier_all, density_all, result, in_sems, out_sems,
):
    size = own.shape[1]
    step = size // 4
    pieces = [(start, half) for start in range(0, size, step) for half in range(2)]
    loads = []
    for k, (start, half) in enumerate(pieces):
        rows = pl.ds(half * size + start, step)
        pair = [
            pltpu.make_async_copy(earlier.at[rows], earlier_all.at[rows], in_sems.at[2 * k]),
            pltpu.make_async_copy(density.at[rows], density_all.at[rows], in_sems.at[2 * k + 1]),
        ]
        for copy in pair:
            copy.start()
        loads.append(pair)
    second = right_occupied[1] == 1
    occupied = (right_occupied[0] + right_occupied[1]).astype(jnp.float32)
    first_flags = [jnp.where(second, a, b) * occupied for a, b in zip(flag_pair(one), flag_pair(own))]
    right_flags = flag_pair(right_next)
    last_flags = [flag * (right_flags[0] + right_flags[1]) for flag in flag_pair(two)]
    stores = []
    for k, (start, half) in enumerate(pieces):
        if half == 0:
            part = pl.ds(start, step)
            first = dot(jnp.where(second, one[part, :], own[part, :]), right_own[:size, :])
            last = dot(two[part, :], right_next[:size, :])
        rows = pl.ds(half * size + start, step)
        for copy in loads[k]:
            copy.wait()
        product = earlier_all[rows, :].astype(jnp.float32) + first_flags[half] * first + last_flags[half] * last
        other = 2.0 * density_all[rows, :].astype(jnp.float32) - product
        value = jnp.where(branch[half] == 1, product, other)
        value = jnp.where(kept[half] == 1, value, 0.0)
        result[rows, :] = value.astype(result.dtype)
        store = pltpu.make_async_copy(result.at[rows], out.at[rows], out_sems.at[k])
        store.start()
        stores.append(store)
    for store in stores:
        store.wait()


def spread_over(rows, axis):
    return lax.all_to_all(rows, axis, 0, 0, tiled=True)


def local(left_panel, right_panel, earlier, density, left_occupied, right_occupied, kept_tiles, branch):
    block_rows, size = left_panel.shape
    row_count, col_count = lax.axis_size("row"), lax.axis_size("col")
    both = ("row", "col")
    left_occupied, right_occupied, kept_tiles = (a.reshape(2) for a in (left_occupied, right_occupied, kept_tiles))
    kind = left_panel.dtype
    payload = jax.ShapeDtypeStruct((size + FLAG_ROWS, size), kind)
    tail = [pltpu.VMEM((FLAG_ROWS, size), kind), pltpu.SemaphoreType.DMA((2,))]

    left_own, wanted = call(
        left_kernel,
        "left",
        [(left_occupied, SMEM), (right_occupied, SMEM), (left_panel, HBM)],
        [payload, jax.ShapeDtypeStruct((8, LANES), jnp.int32)],
        [HBM, VMEM],
        tail,
        LEFT_LIMIT,
    )
    left_one = shift(left_own, "col", -1)

    right_own = call(
        right_kernel, "right", [(right_occupied, SMEM), (right_panel, HBM)], payload, HBM, tail
    )
    to_trace = [
        (((j // 2 + 1) % row_count) * col_count + j, (j // 2) * col_count + (j + 2) % col_count)
        for j in range(col_count)
    ]
    right_trace = lax.ppermute(right_own, both, to_trace)

    to_wanted = [
        (((i + 1) % row_count) * col_count + j, i * col_count + (j + 2) % col_count)
        for i in range(row_count)
        for j in range(col_count)
    ]
    wanted = lax.ppermute(wanted, both, to_wanted)
    right_next = shift(right_own, "row", -1)
    base = call(
        base_kernel,
        "base",
        [(kept_tiles, SMEM), (branch, SMEM), (earlier, HBM), (density, HBM)],
        jax.ShapeDtypeStruct((8, LANES), jnp.float32),
        VMEM,
        [pltpu.VMEM((size, size), kind), pltpu.VMEM((size, size), kind), pltpu.SemaphoreType.DMA((2,))],
    )

    wanted, base = lax.optimization_barrier((wanted, base))

    chosen = jnp.where(wanted[0, 0] == 1, left_one, left_own)
    left_two = shift(chosen, "col", -2)

    parts = call(
        trace_kernel,
        "trace",
        [(right_occupied, SMEM)] + [(a, VMEM) for a in (left_own, left_one, chosen, right_own, right_trace, base)],
        jax.ShapeDtypeStruct((row_count, LANES), jnp.float32),
        VMEM,
    )
    parts = spread_over(parts, "row")
    parts = call(
        middle_kernel, "middle", [(parts, VMEM)], jax.ShapeDtypeStruct((col_count, LANES), jnp.float32), VMEM
    )
    parts = spread_over(parts, "col")
    occupation = call(
        functools.partial(total_kernel, row_count * block_rows),
        "total",
        [(parts, VMEM)],
        jax.ShapeDtypeStruct((1,), jnp.float32),
        SMEM,
    )

    new_density = call(
        last_kernel,
        "last",
        [(right_occupied, SMEM), (kept_tiles, SMEM), (branch, SMEM)]
        + [(a, VMEM) for a in (left_own, left_one, right_own, left_two, right_next)]
        + [(earlier, HBM), (density, HBM)],
        jax.ShapeDtypeStruct((block_rows, size), jnp.bfloat16),
        HBM,
        [pltpu.VMEM((block_rows, size), kind)] * 3
        + [pltpu.SemaphoreType.DMA((16,)), pltpu.SemaphoreType.DMA((8,))],
    )
    return new_density, occupation


def solution(mesh):
    whole = P("row", "col")
    in_specs = (whole,) * 7 + (P("row"),)
    return jax.shard_map(local, mesh=mesh, in_specs=in_specs, out_specs=(whole, P()), check_vma=False)
```

```python
import functools

import jax
import jax.numpy as jnp
from jax import lax
from jax.experimental import pallas as pl
from jax.experimental.pallas import tpu as pltpu
from jax.sharding import PartitionSpec as P

FLAG_ROWS = 16
LANES = 128
PIECES = 4

VMEM = pl.BlockSpec(memory_space=pltpu.VMEM)
SMEM = pl.BlockSpec(memory_space=pltpu.SMEM)
HBM = pl.BlockSpec(memory_space=pltpu.HBM)


def call(kernel, name, ins, outs, out_specs, scratch=(), limit=12 * 2**20):
    return pl.pallas_call(
        kernel,
        out_shape=outs,
        in_specs=[spec for _, spec in ins],
        out_specs=out_specs,
        scratch_shapes=list(scratch),
        compiler_params=pltpu.CompilerParams(vmem_limit_bytes=limit),
        name=name,
    )(*[array for array, _ in ins])


def shift(value, axis, steps):
    count = lax.axis_size(axis)
    return lax.ppermute(value, axis, [(src, (src + steps) % count) for src in range(count)])


def write_flags(occupied, packed):
    size = packed.shape[1]
    lanes = lax.broadcasted_iota(jnp.int32, (FLAG_ROWS, size), 1)
    flags = [occupied[k].astype(jnp.float32) for k in range(2)]
    packed[size:, :] = jnp.where(lanes < size // 2, flags[0], flags[1]).astype(packed.dtype)


def pack_tile(occupied, panel, packed, sem):
    size = panel.shape[1]
    rows = pl.ds(pl.multiple_of(occupied[1] * size, size), size)
    copy = pltpu.make_async_copy(panel.at[rows], packed.at[:size], sem)
    copy.start()
    write_flags(occupied, packed)
    copy.wait()


def left_kernel(occupied, right_occupied, panel, packed, wanted, stage, in_sems, out_sems):
    size = panel.shape[1]
    step = size // PIECES
    loads, stores = [], []
    for k in range(PIECES):
        rows = pl.ds(pl.multiple_of(occupied[1] * size, size) + k * step, step)
        loads.append(pltpu.make_async_copy(panel.at[rows], stage.at[pl.ds(k * step, step)], in_sems.at[k]))
        loads[k].start()
    write_flags(occupied, stage)
    wanted[...] = jnp.full(wanted.shape, right_occupied[1], wanted.dtype)
    for k in range(PIECES):
        loads[k].wait()
        rows = pl.ds(k * step, step if k < PIECES - 1 else step + FLAG_ROWS)
        stores.append(pltpu.make_async_copy(stage.at[rows], packed.at[rows], out_sems.at[k]))
        stores[k].start()
    for store in stores:
        store.wait()


def right_kernel(occupied, panel, packed, sem):
    pack_tile(occupied, panel, packed, sem)


def base_kernel(kept, branch, earlier, density, base, earlier_tile, density_tile, sems):
    size = earlier_tile.shape[0]
    row, col = lax.axis_index("row"), lax.axis_index("col")
    half = lax.rem(col, 2)
    base[...] = jnp.zeros_like(base)

    @pl.when(lax.div(col, 2) == row)
    def _mine():
        rows = pl.ds(pl.multiple_of(half * size, size), size)
        copies = [
            pltpu.make_async_copy(earlier.at[rows], earlier_tile, sems.at[0]),
            pltpu.make_async_copy(density.at[rows], density_tile, sems.at[1]),
        ]
        for copy in copies:
            copy.start()
        for copy in copies:
            copy.wait()
        once = jnp.zeros((1, 1), jnp.float32)
        twice = jnp.zeros((1, 1), jnp.float32)
        for start in range(0, size, LANES):
            part = pl.ds(start, LANES)
            once = once + diagonal(earlier_tile[part, part].astype(jnp.float32))
            twice = twice + diagonal(2.0 * density_tile[part, part].astype(jnp.float32))
        squared = branch[half] == 1
        keep = (kept[half] == 1).astype(jnp.float32)
        lanes = lax.broadcasted_iota(jnp.int32, base.shape, 1)
        value = keep * jnp.where(squared, once, twice - once)
        weight = jnp.where(squared, keep, -keep)
        base[...] = jnp.where(lanes == 0, value, 0.0) + jnp.where(lanes == 2, weight, 0.0)


def flag_pair(payload):
    size = payload.shape[1]
    tail = payload[size:, :].astype(jnp.float32)
    return tail[0:1, 0:1], tail[0:1, size // 2 : size // 2 + 1]


def dot(a, b):
    return jnp.dot(a, b, preferred_element_type=jnp.float32)


def diagonal(block):
    rows = lax.broadcasted_iota(jnp.int32, block.shape, 0)
    cols = lax.broadcasted_iota(jnp.int32, block.shape, 1)
    return jnp.sum(jnp.where(rows == cols, block, 0.0), axis=(0, 1), keepdims=True)


def product_trace(left, right, size):
    total = jnp.zeros((1, 1), jnp.float32)
    for start in range(0, size, LANES):
        part = pl.ds(start, LANES)
        total = total + diagonal(dot(left(part), right[:size, part]))
    return total


def trace_kernel(right_occupied, own, one, chosen, right_own, right_trace, base, parts):
    size = own.shape[1]
    row, col = lax.axis_index("row"), lax.axis_index("col")
    count = lax.axis_size("col")
    half = lax.rem(col, 2)
    lanes = lax.broadcasted_iota(jnp.int32, (1, LANES), 1)
    parts[...] = jnp.zeros_like(parts)

    @pl.when(lax.div(col, 2) == row)
    def _near():
        second = right_occupied[1] == 1
        value = product_trace(lambda part: jnp.where(second, one[part, :], own[part, :]), right_own, size)
        flags = [jnp.where(second, a, b) for a, b in zip(flag_pair(one), flag_pair(own))]
        occupied = (right_occupied[0] + right_occupied[1]).astype(jnp.float32)
        value = value * jnp.where(half == 1, flags[1], flags[0]) * occupied
        known = base[0:1, :]
        weight = jnp.sum(jnp.where(lanes == 2, known, 0.0), axis=1, keepdims=True)
        parts[...] += known + jnp.where(lanes == 0, value * weight, 0.0)

    @pl.when(lax.div(lax.rem(col + count - 2, count), 2) == row)
    def _far():
        value = product_trace(lambda part: chosen[part, :], right_trace, size)
        flags, right_flags = flag_pair(chosen), flag_pair(right_trace)
        value = value * jnp.where(half == 1, flags[1], flags[0]) * (right_flags[0] + right_flags[1])
        parts[...] += jnp.where(lanes == 1, value, 0.0)


def middle_kernel(parts, spread):
    spread[...] = jnp.broadcast_to(jnp.sum(parts[...], axis=0, keepdims=True), spread.shape)


def total_kernel(order, parts, occupation):
    values = parts[...]
    lanes = lax.broadcasted_iota(jnp.int32, values.shape, 1)
    moved = jnp.concatenate([values[-2:], values[:-2]], axis=0)
    weights = jnp.sum(jnp.where(lanes == 2, moved, 0.0), axis=1, keepdims=True)
    far = jnp.sum(jnp.where(lanes == 1, values, 0.0), axis=1, keepdims=True)
    near = jnp.sum(jnp.where(lanes == 0, values, 0.0), axis=1, keepdims=True)
    occupation[0] = jnp.sum(near + weights * far) / order


def last_kernel(
    right_occupied, kept, branch, own, one, right_own, two, right_next, earlier, density, out, result, sems
):
    size = own.shape[1]
    step = size // 4
    second = right_occupied[1] == 1
    occupied = (right_occupied[0] + right_occupied[1]).astype(jnp.float32)
    first_flags = [jnp.where(second, a, b) * occupied for a, b in zip(flag_pair(one), flag_pair(own))]
    right_flags = flag_pair(right_next)
    last_flags = [flag * (right_flags[0] + right_flags[1]) for flag in flag_pair(two)]
    stores = []
    for start in range(0, size, step):
        part = pl.ds(start, step)
        first = dot(jnp.where(second, one[part, :], own[part, :]), right_own[:size, :])
        last = dot(two[part, :], right_next[:size, :])
        for half in range(2):
            rows = pl.ds(half * size + start, step)
            product = earlier[rows, :].astype(jnp.float32) + first_flags[half] * first + last_flags[half] * last
            other = 2.0 * density[rows, :].astype(jnp.float32) - product
            value = jnp.where(branch[half] == 1, product, other)
            value = jnp.where(kept[half] == 1, value, 0.0)
            result[rows, :] = value.astype(result.dtype)
            store = pltpu.make_async_copy(result.at[rows], out.at[rows], sems.at[len(stores)])
            store.start()
            stores.append(store)
    for store in stores:
        store.wait()


def spread_over(rows, axis):
    return lax.all_to_all(rows, axis, 0, 0, tiled=True)


def local(left_panel, right_panel, earlier, density, left_occupied, right_occupied, kept_tiles, branch):
    block_rows, size = left_panel.shape
    row_count, col_count = lax.axis_size("row"), lax.axis_size("col")
    both = ("row", "col")
    left_occupied, right_occupied, kept_tiles = (a.reshape(2) for a in (left_occupied, right_occupied, kept_tiles))
    kind = left_panel.dtype
    payload = jax.ShapeDtypeStruct((size + FLAG_ROWS, size), kind)
    pack_scratch = [pltpu.SemaphoreType.DMA]

    left_own, wanted = call(
        left_kernel,
        "left",
        [(left_occupied, SMEM), (right_occupied, SMEM), (left_panel, HBM)],
        [payload, jax.ShapeDtypeStruct((8, LANES), jnp.int32)],
        [HBM, VMEM],
        [pltpu.VMEM(payload.shape, kind), pltpu.SemaphoreType.DMA((PIECES,)), pltpu.SemaphoreType.DMA((PIECES,))],
        62 * 2**20,
    )
    left_one = shift(left_own, "col", -1)

    right_own = call(
        right_kernel, "right", [(right_occupied, SMEM), (right_panel, HBM)], payload, VMEM, pack_scratch
    )
    to_trace = [
        (((j // 2 + 1) % row_count) * col_count + j, (j // 2) * col_count + (j + 2) % col_count)
        for j in range(col_count)
    ]
    wanted, right_own = lax.optimization_barrier((wanted, right_own))
    right_trace = lax.ppermute(right_own, both, to_trace)
    right_next = shift(right_own, "row", -1)

    to_wanted = [
        (((i + 1) % row_count) * col_count + j, i * col_count + (j + 2) % col_count)
        for i in range(row_count)
        for j in range(col_count)
    ]
    wanted = lax.ppermute(wanted, both, to_wanted)
    base = call(
        base_kernel,
        "base",
        [(kept_tiles, SMEM), (branch, SMEM), (earlier, HBM), (density, HBM)],
        jax.ShapeDtypeStruct((8, LANES), jnp.float32),
        VMEM,
        [pltpu.VMEM((size, size), kind), pltpu.VMEM((size, size), kind), pltpu.SemaphoreType.DMA((2,))],
    )

    wanted, base = lax.optimization_barrier((wanted, base))

    chosen = jnp.where(wanted[0, 0] == 1, left_one, left_own)
    left_two = shift(chosen, "col", -2)

    parts = call(
        trace_kernel,
        "trace",
        [(right_occupied, SMEM)] + [(a, VMEM) for a in (left_own, left_one, chosen, right_own, right_trace, base)],
        jax.ShapeDtypeStruct((row_count, LANES), jnp.float32),
        VMEM,
    )
    parts = spread_over(parts, "row")
    parts = call(
        middle_kernel, "middle", [(parts, VMEM)], jax.ShapeDtypeStruct((col_count, LANES), jnp.float32), VMEM
    )
    parts = spread_over(parts, "col")
    occupation = call(
        functools.partial(total_kernel, row_count * block_rows),
        "total",
        [(parts, VMEM)],
        jax.ShapeDtypeStruct((1,), jnp.float32),
        SMEM,
    )

    new_density = call(
        last_kernel,
        "last",
        [(right_occupied, SMEM), (kept_tiles, SMEM), (branch, SMEM)]
        + [(a, VMEM) for a in (left_own, left_one, right_own, left_two, right_next)]
        + [(earlier, VMEM), (density, VMEM)],
        jax.ShapeDtypeStruct((block_rows, size), jnp.bfloat16),
        HBM,
        [pltpu.VMEM((block_rows, size), kind), pltpu.SemaphoreType.DMA((8,))],
    )
    return new_density, occupation


def solution(mesh):
    whole = P("row", "col")
    in_specs = (whole,) * 7 + (P("row"),)
    return jax.shard_map(local, mesh=mesh, in_specs=in_specs, out_specs=(whole, P()), check_vma=False)
```

```python
import functools

import jax
import jax.numpy as jnp
from jax import lax
from jax.experimental import pallas as pl
from jax.experimental.pallas import tpu as pltpu
from jax.sharding import PartitionSpec as P

FLAG_ROWS = 16
LANES = 128

VMEM = pl.BlockSpec(memory_space=pltpu.VMEM)
SMEM = pl.BlockSpec(memory_space=pltpu.SMEM)
HBM = pl.BlockSpec(memory_space=pltpu.HBM)


def call(kernel, name, ins, outs, out_specs, scratch=(), limit=12 * 2**20):
    return pl.pallas_call(
        kernel,
        out_shape=outs,
        in_specs=[spec for _, spec in ins],
        out_specs=out_specs,
        scratch_shapes=list(scratch),
        compiler_params=pltpu.CompilerParams(vmem_limit_bytes=limit),
        name=name,
    )(*[array for array, _ in ins])


def shift(value, axis, steps):
    count = lax.axis_size(axis)
    return lax.ppermute(value, axis, [(src, (src + steps) % count) for src in range(count)])


def pack_kernel(*refs):
    occupied, panels, packed, (stage, in_sems, out_sems) = refs[:2], refs[2:4], refs[4:6], refs[6:]
    size = stage.shape[2]
    loads, stores = [], []
    for side in range(2):
        rows = pl.ds(pl.multiple_of(occupied[side][1] * size, size), size)
        loads.append(pltpu.make_async_copy(panels[side].at[rows], stage.at[side, :size], in_sems.at[side]))
        loads[side].start()
    for side in range(2):
        lanes = lax.broadcasted_iota(jnp.int32, (FLAG_ROWS, size), 1)
        flags = [occupied[side][k].astype(jnp.float32) for k in range(2)]
        stage[side, size:, :] = jnp.where(lanes < size // 2, flags[0], flags[1]).astype(stage.dtype)
    for side in range(2):
        loads[side].wait()
        stores.append(pltpu.make_async_copy(stage.at[side], packed[side], out_sems.at[side]))
        stores[side].start()
    for store in stores:
        store.wait()


def base_kernel(right_occupied, kept, branch, right_own, earlier, density, base, wanted, right_here, earlier_tile, density_tile, sems):
    size = earlier_tile.shape[0]
    row, col = lax.axis_index(ROW), lax.axis_index(COL)
    half = lax.rem(col, 2)
    base[...] = jnp.zeros_like(base)
    wanted[...] = jnp.full(wanted.shape, right_occupied[1], wanted.dtype)
    right_here[...] = right_own[...]

    @pl.when(lax.div(col, 2) == row)
    def _mine():
        rows = pl.ds(pl.multiple_of(half * size, size), size)
        copies = [
            pltpu.make_async_copy(earlier.at[rows], earlier_tile, sems.at[0]),
            pltpu.make_async_copy(density.at[rows], density_tile, sems.at[1]),
        ]
        for copy in copies:
            copy.start()
        for copy in copies:
            copy.wait()
        once = jnp.zeros((1, 1), jnp.float32)
        twice = jnp.zeros((1, 1), jnp.float32)
        for start in range(0, size, LANES):
            part = pl.ds(start, LANES)
            once = once + diagonal(earlier_tile[part, part].astype(jnp.float32))
            twice = twice + diagonal(2.0 * density_tile[part, part].astype(jnp.float32))
        squared = branch[half] == 1
        keep = (kept[half] == 1).astype(jnp.float32)
        lanes = lax.broadcasted_iota(jnp.int32, base.shape, 1)
        value = keep * jnp.where(squared, once, twice - once)
        weight = jnp.where(squared, keep, -keep)
        high = lax.axis_index("x_hi")
        base[...] = jnp.where(lanes == 0, value, 0.0) + jnp.where(lanes == 3 + high, weight, 0.0)


def flag_pair(payload):
    size = payload.shape[1]
    tail = payload[size:, :].astype(jnp.float32)
    return tail[0:1, 0:1], tail[0:1, size // 2 : size // 2 + 1]


def dot(a, b):
    return jnp.dot(a, b, preferred_element_type=jnp.float32)


def diagonal(block):
    rows = lax.broadcasted_iota(jnp.int32, block.shape, 0)
    cols = lax.broadcasted_iota(jnp.int32, block.shape, 1)
    return jnp.sum(jnp.where(rows == cols, block, 0.0), axis=(0, 1), keepdims=True)


def product_trace(left, right, size):
    total = jnp.zeros((1, 1), jnp.float32)
    for start in range(0, size, LANES):
        part = pl.ds(start, LANES)
        total = total + diagonal(dot(left(part), right[:size, part]))
    return total


def far_here():
    row, col = lax.axis_index(ROW), lax.axis_index(COL)
    count = lax.axis_size(COL)
    return lax.div(lax.rem(col + count - 2, count), 2) == row


def decide_kernel(wanted, right_trace, second):
    second[...] = wanted[...]

    @pl.when(far_here())
    def _far():
        flag = flag_pair(right_trace)[1].astype(second.dtype)
        second[...] = jnp.broadcast_to(flag, second.shape)


def choose_kernel(second, own, one, chosen):
    use_one = jnp.max(second[...]) == 1

    @pl.when(use_one)
    def _one():
        chosen[...] = one[...]

    @pl.when(jnp.logical_not(use_one))
    def _own():
        chosen[...] = own[...]


def trace_kernel(right_occupied, own, one, chosen, right_own, right_trace, base, parts):
    size = own.shape[1]
    row, col = lax.axis_index(ROW), lax.axis_index(COL)
    half = lax.rem(col, 2)
    lanes = lax.broadcasted_iota(jnp.int32, (1, LANES), 1)
    parts[...] = jnp.zeros_like(parts)

    @pl.when(lax.div(col, 2) == row)
    def _near():
        second = right_occupied[1] == 1
        value = product_trace(lambda part: jnp.where(second, one[part, :], own[part, :]), right_own, size)
        flags = [jnp.where(second, a, b) for a, b in zip(flag_pair(one), flag_pair(own))]
        occupied = (right_occupied[0] + right_occupied[1]).astype(jnp.float32)
        value = value * jnp.where(half == 1, flags[1], flags[0]) * occupied
        known = base[0:1, :]
        weight = jnp.sum(jnp.where(lanes == 3 + lax.axis_index("x_hi"), known, 0.0), axis=1, keepdims=True)
        parts[...] += known + jnp.where(lanes == 0, value * weight, 0.0)

    @pl.when(far_here())
    def _far():
        value = product_trace(lambda part: chosen[part, :], right_trace, size)
        flags, right_flags = flag_pair(chosen), flag_pair(right_trace)
        value = value * jnp.where(half == 1, flags[1], flags[0]) * (right_flags[0] + right_flags[1])
        parts[...] += jnp.where(lanes == 1 + lax.axis_index("x_hi"), value, 0.0)


def middle_kernel(parts, spread):
    spread[...] = jnp.broadcast_to(jnp.sum(parts[...], axis=0, keepdims=True), spread.shape)


def total_kernel(order, parts, occupation):
    values = parts[...]
    lanes = lax.broadcasted_iota(jnp.int32, values.shape, 1)
    planes = lax.broadcasted_iota(jnp.int32, (values.shape[0], 1), 0)
    moved = jnp.concatenate([values[-2:], values[:-2]], axis=0)

    def lane(array, index):
        return jnp.sum(jnp.where(lanes == index, array, 0.0), axis=1, keepdims=True)

    low, high = lane(moved, 3), lane(moved, 4)
    low, high = jnp.where(planes < 2, high, low), jnp.where(planes < 2, low, high)
    occupation[0] = jnp.sum(lane(values, 0) + lane(values, 1) * low + lane(values, 2) * high) / order


def last_kernel(
    right_occupied, kept, branch, own, one, right_own, two, right_next, earlier, density, out, result, sems
):
    size = own.shape[1]
    step = size // 4
    second = right_occupied[1] == 1
    occupied = (right_occupied[0] + right_occupied[1]).astype(jnp.float32)
    first_flags = [jnp.where(second, a, b) * occupied for a, b in zip(flag_pair(one), flag_pair(own))]
    right_flags = flag_pair(right_next)
    last_flags = [flag * (right_flags[0] + right_flags[1]) for flag in flag_pair(two)]
    signs = [jnp.where(branch[half] == 1, 1.0, -1.0) for half in range(2)]
    stores = []
    for start in range(0, size, step):
        part = pl.ds(start, step)
        first = dot(jnp.where(second, one[part, :], own[part, :]), right_own[:size, :])
        last = dot(two[part, :], right_next[:size, :])
        for half in range(2):
            rows = pl.ds(half * size + start, step)
            product = earlier[rows, :].astype(jnp.float32) + first_flags[half] * first + last_flags[half] * last
            value = signs[half] * product + (1.0 - signs[half]) * density[rows, :].astype(jnp.float32)
            value = jnp.where(kept[half] == 1, value, 0.0)
            result[rows, :] = value.astype(result.dtype)
            store = pltpu.make_async_copy(result.at[rows], out.at[rows], sems.at[len(stores)])
            store.start()
            stores.append(store)
    for store in stores:
        store.wait()


def spread_over(rows, axis):
    return lax.all_to_all(rows, axis, 0, 0, tiled=True)


AXES = ("y", "x_lo", "core", "x_hi", "z")
SIZES = (4, 2, 2, 2, 16)
ROW, COL, PLANE = AXES[:3], AXES[3:], AXES[:4]


def local(left_panel, right_panel, earlier, density, left_occupied, right_occupied, kept_tiles, branch):
    block_rows, size = left_panel.shape
    row_count, col_count = lax.axis_size(ROW), lax.axis_size(COL)
    both = AXES
    left_occupied, right_occupied, kept_tiles = (a.reshape(2) for a in (left_occupied, right_occupied, kept_tiles))
    kind = left_panel.dtype
    payload = jax.ShapeDtypeStruct((size + FLAG_ROWS, size), kind)

    left_own, right_own = call(
        pack_kernel,
        "pack",
        [(left_occupied, SMEM), (right_occupied, SMEM), (left_panel, HBM), (right_panel, HBM)],
        [payload, payload],
        [HBM, HBM],
        [pltpu.VMEM((2,) + payload.shape, kind), pltpu.SemaphoreType.DMA((2,)), pltpu.SemaphoreType.DMA((2,))],
        62 * 2**20,
    )
    left_one = shift(left_own, COL, -1)

    to_trace = [
        (((j // 2 + 1) % row_count) * col_count + j, (j // 2) * col_count + (j + 2) % col_count)
        for j in range(col_count)
    ]
    right_trace = lax.ppermute(right_own, both, to_trace)

    base, wanted, right_here = call(
        base_kernel,
        "base",
        [(right_occupied, SMEM), (kept_tiles, SMEM), (branch, SMEM), (right_own, VMEM), (earlier, HBM), (density, HBM)],
        [jax.ShapeDtypeStruct((8, LANES), jnp.float32), jax.ShapeDtypeStruct((8, LANES), jnp.int32), payload],
        [VMEM, VMEM, VMEM],
        [pltpu.VMEM((size, size), kind), pltpu.VMEM((size, size), kind), pltpu.SemaphoreType.DMA((2,))],
    )

    to_wanted = [
        (((i + 1) % row_count) * col_count + j, i * col_count + (j + 2) % col_count)
        for i in range(row_count)
        for j in range(col_count)
        if j // 2 != i
    ]
    wanted = lax.ppermute(wanted, both, to_wanted)
    right_next = shift(right_here, ROW, -1)

    second = call(
        decide_kernel,
        "decide",
        [(wanted, VMEM), (right_trace, VMEM)],
        jax.ShapeDtypeStruct((8, LANES), jnp.int32),
        VMEM,
    )
    chosen = call(choose_kernel, "choose", [(a, VMEM) for a in (second, left_own, left_one)], payload, VMEM)
    left_two = shift(chosen, COL, -2)

    parts = call(
        trace_kernel,
        "trace",
        [(right_occupied, SMEM)] + [(a, VMEM) for a in (left_own, left_one, chosen, right_here, right_trace, base)],
        jax.ShapeDtypeStruct((lax.axis_size(PLANE), LANES), jnp.float32),
        VMEM,
    )
    parts = spread_over(parts, PLANE)
    parts = call(
        middle_kernel, "middle", [(parts, VMEM)], jax.ShapeDtypeStruct((lax.axis_size("z"), LANES), jnp.float32), VMEM
    )
    parts = spread_over(parts, "z")
    occupation = call(
        functools.partial(total_kernel, row_count * block_rows),
        "total",
        [(parts, VMEM)],
        jax.ShapeDtypeStruct((1,), jnp.float32),
        SMEM,
    )

    new_density = call(
        last_kernel,
        "last",
        [(right_occupied, SMEM), (kept_tiles, SMEM), (branch, SMEM)]
        + [(a, VMEM) for a in (left_own, left_one, right_here, left_two, right_next, earlier, density)],
        jax.ShapeDtypeStruct((block_rows, size), jnp.bfloat16),
        HBM,
        [pltpu.VMEM((block_rows, size), kind), pltpu.SemaphoreType.DMA((8,))],
    )
    return new_density, occupation


def solution(mesh):
    mesh = jax.sharding.Mesh(mesh.devices.reshape(SIZES), AXES)
    whole = P(ROW, COL)
    in_specs = (whole,) * 7 + (P(ROW),)
    return jax.shard_map(local, mesh=mesh, in_specs=in_specs, out_specs=(whole, P()), check_vma=False)
```

```python
import functools

import jax
import jax.numpy as jnp
from jax import lax
from jax.experimental import pallas as pl
from jax.experimental.pallas import tpu as pltpu
from jax.sharding import PartitionSpec as P

FLAG_ROWS = 16
LANES = 128

VMEM = pl.BlockSpec(memory_space=pltpu.VMEM)
SMEM = pl.BlockSpec(memory_space=pltpu.SMEM)
HBM = pl.BlockSpec(memory_space=pltpu.HBM)


def call(kernel, name, ins, outs, out_specs, scratch=(), limit=12 * 2**20):
    return pl.pallas_call(
        kernel,
        out_shape=outs,
        in_specs=[spec for _, spec in ins],
        out_specs=out_specs,
        scratch_shapes=list(scratch),
        compiler_params=pltpu.CompilerParams(vmem_limit_bytes=limit),
        name=name,
    )(*[array for array, _ in ins])


def shift(value, axis, steps):
    count = lax.axis_size(axis)
    return lax.ppermute(value, axis, [(src, (src + steps) % count) for src in range(count)])


def pack_kernel(*refs):
    occupied, panels, packed, (stage, flags, in_sems, out_sems, flag_sems) = refs[:2], refs[2:4], refs[4:6], refs[6:]
    size = stage.shape[3]
    asked = [pltpu.make_async_copy(occupied[side], flags.at[side], flag_sems.at[side]) for side in range(2)]
    loads = [
        pltpu.make_async_copy(panels[side].at[pl.ds(half * size, size)], stage.at[side, half, :size], in_sems.at[side, half])
        for side in range(2)
        for half in range(2)
    ]
    for copy in asked + loads:
        copy.start()
    for side in range(2):
        asked[side].wait()
        lanes = lax.broadcasted_iota(jnp.int32, (FLAG_ROWS, size), 1)
        values = [flags[side, k].astype(jnp.float32) for k in range(2)]
        rows = jnp.where(lanes < size // 2, values[0], values[1]).astype(stage.dtype)
        for half in range(2):
            stage[side, half, size:, :] = rows
    for copy in loads:
        copy.wait()
    stores = [
        pltpu.make_async_copy(stage.at[side, flags[side, 1]], packed[side], out_sems.at[side]) for side in range(2)
    ]
    for store in stores:
        store.start()
    for store in stores:
        store.wait()


def base_kernel(right_occupied, kept, branch, right_own, earlier, density, base, wanted, right_here, earlier_tile, density_tile, sems):
    size = earlier_tile.shape[0]
    row, col = lax.axis_index(ROW), lax.axis_index(COL)
    half = lax.rem(col, 2)
    base[...] = jnp.zeros_like(base)
    wanted[...] = jnp.full(wanted.shape, right_occupied[1], wanted.dtype)
    right_here[...] = right_own[...]

    @pl.when(lax.div(col, 2) == row)
    def _mine():
        rows = pl.ds(pl.multiple_of(half * size, size), size)
        copies = [
            pltpu.make_async_copy(earlier.at[rows], earlier_tile, sems.at[0]),
            pltpu.make_async_copy(density.at[rows], density_tile, sems.at[1]),
        ]
        for copy in copies:
            copy.start()
        for copy in copies:
            copy.wait()
        once = jnp.zeros((1, 1), jnp.float32)
        twice = jnp.zeros((1, 1), jnp.float32)
        for start in range(0, size, LANES):
            part = pl.ds(start, LANES)
            once = once + diagonal(earlier_tile[part, part].astype(jnp.float32))
            twice = twice + diagonal(2.0 * density_tile[part, part].astype(jnp.float32))
        squared = branch[half] == 1
        keep = (kept[half] == 1).astype(jnp.float32)
        lanes = lax.broadcasted_iota(jnp.int32, base.shape, 1)
        value = keep * jnp.where(squared, once, twice - once)
        weight = jnp.where(squared, keep, -keep)
        high = lax.axis_index("x_hi")
        base[...] = jnp.where(lanes == 0, value, 0.0) + jnp.where(lanes == 3 + high, weight, 0.0)


def flag_pair(payload):
    size = payload.shape[1]
    tail = payload[size:, :].astype(jnp.float32)
    return tail[0:1, 0:1], tail[0:1, size // 2 : size // 2 + 1]


def dot(a, b):
    return jnp.dot(a, b, preferred_element_type=jnp.float32)


def diagonal(block):
    rows = lax.broadcasted_iota(jnp.int32, block.shape, 0)
    cols = lax.broadcasted_iota(jnp.int32, block.shape, 1)
    return jnp.sum(jnp.where(rows == cols, block, 0.0), axis=(0, 1), keepdims=True)


def product_trace(left, right, size):
    total = jnp.zeros((1, 1), jnp.float32)
    for start in range(0, size, LANES):
        part = pl.ds(start, LANES)
        total = total + diagonal(dot(left(part), right[:size, part]))
    return total


def far_here():
    row, col = lax.axis_index(ROW), lax.axis_index(COL)
    count = lax.axis_size(COL)
    return lax.div(lax.rem(col + count - 2, count), 2) == row


def decide_kernel(wanted, right_trace, second):
    second[...] = wanted[...]

    @pl.when(far_here())
    def _far():
        flag = flag_pair(right_trace)[1].astype(second.dtype)
        second[...] = jnp.broadcast_to(flag, second.shape)


def choose_kernel(second, own, one, chosen):
    use_one = jnp.max(second[...]) == 1

    @pl.when(use_one)
    def _one():
        chosen[...] = one[...]

    @pl.when(jnp.logical_not(use_one))
    def _own():
        chosen[...] = own[...]


def trace_kernel(right_occupied, own, one, chosen, right_own, right_trace, base, parts):
    size = own.shape[1]
    row, col = lax.axis_index(ROW), lax.axis_index(COL)
    half = lax.rem(col, 2)
    lanes = lax.broadcasted_iota(jnp.int32, (1, LANES), 1)
    parts[...] = jnp.zeros_like(parts)

    @pl.when(lax.div(col, 2) == row)
    def _near():
        second = right_occupied[1] == 1
        value = product_trace(lambda part: jnp.where(second, one[part, :], own[part, :]), right_own, size)
        flags = [jnp.where(second, a, b) for a, b in zip(flag_pair(one), flag_pair(own))]
        occupied = (right_occupied[0] + right_occupied[1]).astype(jnp.float32)
        value = value * jnp.where(half == 1, flags[1], flags[0]) * occupied
        known = base[0:1, :]
        weight = jnp.sum(jnp.where(lanes == 3 + lax.axis_index("x_hi"), known, 0.0), axis=1, keepdims=True)
        parts[...] += known + jnp.where(lanes == 0, value * weight, 0.0)

    @pl.when(far_here())
    def _far():
        value = product_trace(lambda part: chosen[part, :], right_trace, size)
        flags, right_flags = flag_pair(chosen), flag_pair(right_trace)
        value = value * jnp.where(half == 1, flags[1], flags[0]) * (right_flags[0] + right_flags[1])
        parts[...] += jnp.where(lanes == 1 + lax.axis_index("x_hi"), value, 0.0)


def middle_kernel(parts, spread):
    spread[...] = jnp.broadcast_to(jnp.sum(parts[...], axis=0, keepdims=True), spread.shape)


def total_kernel(order, parts, stored, occupation):
    values = parts[...]
    lanes = lax.broadcasted_iota(jnp.int32, values.shape, 1)
    planes = lax.broadcasted_iota(jnp.int32, (values.shape[0], 1), 0)
    moved = jnp.concatenate([values[-2:], values[:-2]], axis=0)

    def lane(array, index):
        return jnp.sum(jnp.where(lanes == index, array, 0.0), axis=1, keepdims=True)

    low, high = lane(moved, 3), lane(moved, 4)
    low, high = jnp.where(planes < 2, high, low), jnp.where(planes < 2, low, high)
    occupation[0] = jnp.sum(lane(values, 0) + lane(values, 1) * low + lane(values, 2) * high) / order


def last_kernel(
    right_occupied, kept, branch, own, one, right_own, two, right_next, earlier, density, out, stored, result, sems
):
    size = own.shape[1]
    step = size // 4
    stored[...] = jnp.zeros_like(stored)
    second = right_occupied[1] == 1
    occupied = (right_occupied[0] + right_occupied[1]).astype(jnp.float32)
    first_flags = [jnp.where(second, a, b) * occupied for a, b in zip(flag_pair(one), flag_pair(own))]
    right_flags = flag_pair(right_next)
    last_flags = [flag * (right_flags[0] + right_flags[1]) for flag in flag_pair(two)]
    signs = [jnp.where(branch[half] == 1, 1.0, -1.0) for half in range(2)]
    stores = []
    for start in range(0, size, step):
        part = pl.ds(start, step)
        first = dot(jnp.where(second, one[part, :], own[part, :]), right_own[:size, :])
        last = dot(two[part, :], right_next[:size, :])
        for half in range(2):
            rows = pl.ds(half * size + start, step)
            product = earlier[rows, :].astype(jnp.float32) + first_flags[half] * first + last_flags[half] * last
            value = signs[half] * product + (1.0 - signs[half]) * density[rows, :].astype(jnp.float32)
            value = jnp.where(kept[half] == 1, value, 0.0)
            result[rows, :] = value.astype(result.dtype)
            store = pltpu.make_async_copy(result.at[rows], out.at[rows], sems.at[len(stores)])
            store.start()
            stores.append(store)
    for store in stores:
        store.wait()


def spread_over(rows, axis):
    return lax.all_to_all(rows, axis, 0, 0, tiled=True)


AXES = ("y", "x_lo", "core", "x_hi", "z")
SIZES = (4, 2, 2, 2, 16)
ROW, COL, PLANE = AXES[:3], AXES[3:], AXES[:4]


def local(left_panel, right_panel, earlier, density, left_occupied, right_occupied, kept_tiles, branch):
    block_rows, size = left_panel.shape
    row_count, col_count = lax.axis_size(ROW), lax.axis_size(COL)
    both = AXES
    left_occupied, right_occupied, kept_tiles = (a.reshape(2) for a in (left_occupied, right_occupied, kept_tiles))
    kind = left_panel.dtype
    payload = jax.ShapeDtypeStruct((size + FLAG_ROWS, size), kind)

    left_own, right_own = call(
        pack_kernel,
        "pack",
        [(left_occupied, HBM), (right_occupied, HBM), (left_panel, HBM), (right_panel, HBM)],
        [payload, payload],
        [HBM, HBM],
        [
            pltpu.VMEM((2, 2) + payload.shape, kind),
            pltpu.SMEM((2, 2), jnp.int32),
            pltpu.SemaphoreType.DMA((2, 2)),
            pltpu.SemaphoreType.DMA((2,)),
            pltpu.SemaphoreType.DMA((2,)),
        ],
        62 * 2**20,
    )
    left_one = shift(left_own, COL, -1)

    to_trace = [
        (((j // 2 + 1) % row_count) * col_count + j, (j // 2) * col_count + (j + 2) % col_count)
        for j in range(col_count)
    ]
    right_trace = lax.ppermute(right_own, both, to_trace)

    base, wanted, right_here = call(
        base_kernel,
        "base",
        [(right_occupied, SMEM), (kept_tiles, SMEM), (branch, SMEM), (right_own, VMEM), (earlier, HBM), (density, HBM)],
        [jax.ShapeDtypeStruct((8, LANES), jnp.float32), jax.ShapeDtypeStruct((8, LANES), jnp.int32), payload],
        [VMEM, VMEM, VMEM],
        [pltpu.VMEM((size, size), kind), pltpu.VMEM((size, size), kind), pltpu.SemaphoreType.DMA((2,))],
    )

    to_wanted = [
        (((i + 1) % row_count) * col_count + j, i * col_count + (j + 2) % col_count)
        for i in range(row_count)
        for j in range(col_count)
        if j // 2 != i
    ]
    wanted = lax.ppermute(wanted, both, to_wanted)
    right_next = shift(right_own, ROW, -1)

    second = call(
        decide_kernel,
        "decide",
        [(wanted, VMEM), (right_trace, VMEM)],
        jax.ShapeDtypeStruct((8, LANES), jnp.int32),
        VMEM,
    )
    chosen = call(choose_kernel, "choose", [(a, VMEM) for a in (second, left_own, left_one)], payload, VMEM)
    left_two = shift(chosen, COL, -2)

    parts = call(
        trace_kernel,
        "trace",
        [(right_occupied, SMEM)] + [(a, VMEM) for a in (left_own, left_one, chosen, right_here, right_trace, base)],
        jax.ShapeDtypeStruct((lax.axis_size(PLANE), LANES), jnp.float32),
        VMEM,
    )
    parts = spread_over(parts, PLANE)
    parts = call(
        middle_kernel, "middle", [(parts, VMEM)], jax.ShapeDtypeStruct((lax.axis_size("z"), LANES), jnp.float32), VMEM
    )
    parts = spread_over(parts, "z")
    new_density, stored = call(
        last_kernel,
        "last",
        [(right_occupied, SMEM), (kept_tiles, SMEM), (branch, SMEM)]
        + [(a, VMEM) for a in (left_own, left_one, right_own, left_two, right_next, earlier, density)],
        [jax.ShapeDtypeStruct((block_rows, size), jnp.bfloat16), jax.ShapeDtypeStruct((8, LANES), jnp.float32)],
        [HBM, VMEM],
        [pltpu.VMEM((block_rows, size), kind), pltpu.SemaphoreType.DMA((8,))],
    )

    occupation = call(
        functools.partial(total_kernel, row_count * block_rows),
        "total",
        [(parts, VMEM), (stored, VMEM)],
        jax.ShapeDtypeStruct((1,), jnp.float32),
        SMEM,
    )
    return new_density, occupation


def solution(mesh):
    mesh = jax.sharding.Mesh(mesh.devices.reshape(SIZES), AXES)
    whole = P(ROW, COL)
    in_specs = (whole,) * 7 + (P(ROW),)
    return jax.shard_map(local, mesh=mesh, in_specs=in_specs, out_specs=(whole, P()), check_vma=False)
```

```python
import functools

import jax
import jax.numpy as jnp
from jax import lax
from jax.experimental import pallas as pl
from jax.experimental.pallas import tpu as pltpu
from jax.sharding import PartitionSpec as P

FLAG_ROWS = 16
LANES = 128

VMEM = pl.BlockSpec(memory_space=pltpu.VMEM)
SMEM = pl.BlockSpec(memory_space=pltpu.SMEM)
HBM = pl.BlockSpec(memory_space=pltpu.HBM)


def call(kernel, name, ins, outs, out_specs, scratch=(), limit=12 * 2**20):
    return pl.pallas_call(
        kernel,
        out_shape=outs,
        in_specs=[spec for _, spec in ins],
        out_specs=out_specs,
        scratch_shapes=list(scratch),
        compiler_params=pltpu.CompilerParams(vmem_limit_bytes=limit),
        name=name,
    )(*[array for array, _ in ins])


def shift(value, axis, steps):
    count = lax.axis_size(axis)
    return lax.ppermute(value, axis, [(src, (src + steps) % count) for src in range(count)])


def pack_kernel(*refs):
    occupied, panels, packed, (stage, flags, in_sems, out_sems, flag_sems) = refs[:2], refs[2:4], refs[4:6], refs[6:]
    size = stage.shape[3]
    asked = [pltpu.make_async_copy(occupied[side], flags.at[side], flag_sems.at[side]) for side in range(2)]
    loads = [
        pltpu.make_async_copy(panels[side].at[pl.ds(half * size, size)], stage.at[side, half, :size], in_sems.at[side, half])
        for side in range(2)
        for half in range(2)
    ]
    for copy in asked + loads:
        copy.start()
    for side in range(2):
        asked[side].wait()
        lanes = lax.broadcasted_iota(jnp.int32, (FLAG_ROWS, size), 1)
        values = [flags[side, k].astype(jnp.float32) for k in range(2)]
        rows = jnp.where(lanes < size // 2, values[0], values[1]).astype(stage.dtype)
        for half in range(2):
            stage[side, half, size:, :] = rows
    for copy in loads:
        copy.wait()
    stores = [
        pltpu.make_async_copy(stage.at[side, flags[side, 1]], packed[side], out_sems.at[side]) for side in range(2)
    ]
    for store in stores:
        store.start()
    for store in stores:
        store.wait()


def base_kernel(right_occupied, kept, branch, right_own, earlier, density, base, wanted, right_here, earlier_tile, density_tile, sems):
    size = earlier_tile.shape[0]
    row, col = lax.axis_index(ROW), lax.axis_index(COL)
    half = lax.rem(col, 2)
    base[...] = jnp.zeros_like(base)
    wanted[...] = jnp.full(wanted.shape, right_occupied[1], wanted.dtype)
    right_here[...] = right_own[...]

    @pl.when(lax.div(col, 2) == row)
    def _mine():
        rows = pl.ds(pl.multiple_of(half * size, size), size)
        copies = [
            pltpu.make_async_copy(earlier.at[rows], earlier_tile, sems.at[0]),
            pltpu.make_async_copy(density.at[rows], density_tile, sems.at[1]),
        ]
        for copy in copies:
            copy.start()
        for copy in copies:
            copy.wait()
        once = jnp.zeros((1, 1), jnp.float32)
        twice = jnp.zeros((1, 1), jnp.float32)
        for start in range(0, size, LANES):
            part = pl.ds(start, LANES)
            once = once + diagonal(earlier_tile[part, part].astype(jnp.float32))
            twice = twice + diagonal(2.0 * density_tile[part, part].astype(jnp.float32))
        squared = branch[half] == 1
        keep = (kept[half] == 1).astype(jnp.float32)
        lanes = lax.broadcasted_iota(jnp.int32, base.shape, 1)
        value = keep * jnp.where(squared, once, twice - once)
        weight = jnp.where(squared, keep, -keep)
        high = lax.axis_index("x_hi")
        base[...] = jnp.where(lanes == 0, value, 0.0) + jnp.where(lanes == 3 + high, weight, 0.0)


def flag_pair(payload):
    size = payload.shape[1]
    tail = payload[size:, :].astype(jnp.float32)
    return tail[0:1, 0:1], tail[0:1, size // 2 : size // 2 + 1]


def dot(a, b):
    return jnp.dot(a, b, preferred_element_type=jnp.float32)


def diagonal(block):
    rows = lax.broadcasted_iota(jnp.int32, block.shape, 0)
    cols = lax.broadcasted_iota(jnp.int32, block.shape, 1)
    return jnp.sum(jnp.where(rows == cols, block, 0.0), axis=(0, 1), keepdims=True)


def product_trace(left, right, size):
    total = jnp.zeros((1, 1), jnp.float32)
    for start in range(0, size, LANES):
        part = pl.ds(start, LANES)
        total = total + diagonal(dot(left(part), right[:size, part]))
    return total


def far_here():
    row, col = lax.axis_index(ROW), lax.axis_index(COL)
    count = lax.axis_size(COL)
    return lax.div(lax.rem(col + count - 2, count), 2) == row


def decide_kernel(wanted, right_trace, second):
    second[...] = wanted[...]

    @pl.when(far_here())
    def _far():
        flag = flag_pair(right_trace)[1].astype(second.dtype)
        second[...] = jnp.broadcast_to(flag, second.shape)


def choose_kernel(second, own, one, parts, chosen):
    use_one = jnp.max(second[...]) == 1

    @pl.when(use_one)
    def _one():
        chosen[...] = one[...]

    @pl.when(jnp.logical_not(use_one))
    def _own():
        chosen[...] = own[...]


def trace_kernel(right_occupied, own, one, right_own, right_trace, base, parts):
    size = own.shape[1]
    row, col = lax.axis_index(ROW), lax.axis_index(COL)
    half = lax.rem(col, 2)
    lanes = lax.broadcasted_iota(jnp.int32, (1, LANES), 1)
    parts[...] = jnp.zeros_like(parts)

    @pl.when(lax.div(col, 2) == row)
    def _near():
        second = right_occupied[1] == 1
        value = product_trace(lambda part: jnp.where(second, one[part, :], own[part, :]), right_own, size)
        flags = [jnp.where(second, a, b) for a, b in zip(flag_pair(one), flag_pair(own))]
        occupied = (right_occupied[0] + right_occupied[1]).astype(jnp.float32)
        value = value * jnp.where(half == 1, flags[1], flags[0]) * occupied
        known = base[0:1, :]
        weight = jnp.sum(jnp.where(lanes == 3 + lax.axis_index("x_hi"), known, 0.0), axis=1, keepdims=True)
        parts[...] += known + jnp.where(lanes == 0, value * weight, 0.0)

    @pl.when(far_here())
    def _far():
        right_flags = flag_pair(right_trace)
        second = jnp.max(right_flags[1]) == 1.0
        value = product_trace(lambda part: jnp.where(second, one[part, :], own[part, :]), right_trace, size)
        flags = [jnp.where(second, a, b) for a, b in zip(flag_pair(one), flag_pair(own))]
        value = value * jnp.where(half == 1, flags[1], flags[0]) * (right_flags[0] + right_flags[1])
        parts[...] += jnp.where(lanes == 1 + lax.axis_index("x_hi"), value, 0.0)


def middle_kernel(parts, spread):
    spread[...] = jnp.broadcast_to(jnp.sum(parts[...], axis=0, keepdims=True), spread.shape)


def total_kernel(order, parts, stored, occupation):
    values = parts[...]
    lanes = lax.broadcasted_iota(jnp.int32, values.shape, 1)
    planes = lax.broadcasted_iota(jnp.int32, (values.shape[0], 1), 0)
    moved = jnp.concatenate([values[-2:], values[:-2]], axis=0)

    def lane(array, index):
        return jnp.sum(jnp.where(lanes == index, array, 0.0), axis=1, keepdims=True)

    low, high = lane(moved, 3), lane(moved, 4)
    low, high = jnp.where(planes < 2, high, low), jnp.where(planes < 2, low, high)
    occupation[0] = jnp.sum(lane(values, 0) + lane(values, 1) * low + lane(values, 2) * high) / order


def last_kernel(
    right_occupied, kept, branch, own, one, right_own, two, right_next, earlier, density, out, stored, result, sems
):
    size = own.shape[1]
    step = size // 4
    stored[...] = jnp.zeros_like(stored)
    second = right_occupied[1] == 1
    occupied = (right_occupied[0] + right_occupied[1]).astype(jnp.float32)
    first_flags = [jnp.where(second, a, b) * occupied for a, b in zip(flag_pair(one), flag_pair(own))]
    right_flags = flag_pair(right_next)
    last_flags = [flag * (right_flags[0] + right_flags[1]) for flag in flag_pair(two)]
    signs = [jnp.where(branch[half] == 1, 1.0, -1.0) for half in range(2)]
    stores = []
    for start in range(0, size, step):
        part = pl.ds(start, step)
        first = dot(jnp.where(second, one[part, :], own[part, :]), right_own[:size, :])
        last = dot(two[part, :], right_next[:size, :])
        for half in range(2):
            rows = pl.ds(half * size + start, step)
            product = earlier[rows, :].astype(jnp.float32) + first_flags[half] * first + last_flags[half] * last
            value = signs[half] * product + (1.0 - signs[half]) * density[rows, :].astype(jnp.float32)
            value = jnp.where(kept[half] == 1, value, 0.0)
            result[rows, :] = value.astype(result.dtype)
            store = pltpu.make_async_copy(result.at[rows], out.at[rows], sems.at[len(stores)])
            store.start()
            stores.append(store)
    for store in stores:
        store.wait()


def spread_over(rows, axis):
    return lax.all_to_all(rows, axis, 0, 0, tiled=True)


AXES = ("y", "x_lo", "core", "x_hi", "z")
SIZES = (4, 2, 2, 2, 16)
ROW, COL, PLANE = AXES[:3], AXES[3:], AXES[:4]


def local(left_panel, right_panel, earlier, density, left_occupied, right_occupied, kept_tiles, branch):
    block_rows, size = left_panel.shape
    row_count, col_count = lax.axis_size(ROW), lax.axis_size(COL)
    both = AXES
    left_occupied, right_occupied, kept_tiles = (a.reshape(2) for a in (left_occupied, right_occupied, kept_tiles))
    kind = left_panel.dtype
    payload = jax.ShapeDtypeStruct((size + FLAG_ROWS, size), kind)

    left_own, right_own = call(
        pack_kernel,
        "pack",
        [(left_occupied, HBM), (right_occupied, HBM), (left_panel, HBM), (right_panel, HBM)],
        [payload, payload],
        [HBM, HBM],
        [
            pltpu.VMEM((2, 2) + payload.shape, kind),
            pltpu.SMEM((2, 2), jnp.int32),
            pltpu.SemaphoreType.DMA((2, 2)),
            pltpu.SemaphoreType.DMA((2,)),
            pltpu.SemaphoreType.DMA((2,)),
        ],
        62 * 2**20,
    )
    left_one = shift(left_own, COL, -1)

    to_trace = [
        (((j // 2 + 1) % row_count) * col_count + j, (j // 2) * col_count + (j + 2) % col_count)
        for j in range(col_count)
    ]
    right_trace = lax.ppermute(right_own, both, to_trace)

    base, wanted, right_here = call(
        base_kernel,
        "base",
        [(right_occupied, SMEM), (kept_tiles, SMEM), (branch, SMEM), (right_own, VMEM), (earlier, HBM), (density, HBM)],
        [jax.ShapeDtypeStruct((8, LANES), jnp.float32), jax.ShapeDtypeStruct((8, LANES), jnp.int32), payload],
        [VMEM, VMEM, VMEM],
        [pltpu.VMEM((size, size), kind), pltpu.VMEM((size, size), kind), pltpu.SemaphoreType.DMA((2,))],
    )

    to_wanted = [
        (((i + 1) % row_count) * col_count + j, i * col_count + (j + 2) % col_count)
        for i in range(row_count)
        for j in range(col_count)
        if j // 2 != i
    ]
    wanted = lax.ppermute(wanted, both, to_wanted)
    right_next = shift(right_own, ROW, -1)

    second = call(
        decide_kernel,
        "decide",
        [(wanted, VMEM), (right_trace, VMEM)],
        jax.ShapeDtypeStruct((8, LANES), jnp.int32),
        VMEM,
    )
    parts = call(
        trace_kernel,
        "trace",
        [(right_occupied, SMEM)] + [(a, VMEM) for a in (left_own, left_one, right_here, right_trace, base)],
        jax.ShapeDtypeStruct((lax.axis_size(PLANE), LANES), jnp.float32),
        VMEM,
    )

    chosen = call(choose_kernel, "choose", [(a, VMEM) for a in (second, left_own, left_one, parts)], payload, VMEM)
    left_two = shift(chosen, COL, -2)
    parts = spread_over(parts, PLANE)
    parts = call(
        middle_kernel, "middle", [(parts, VMEM)], jax.ShapeDtypeStruct((lax.axis_size("z"), LANES), jnp.float32), VMEM
    )
    parts = spread_over(parts, "z")
    new_density, stored = call(
        last_kernel,
        "last",
        [(right_occupied, SMEM), (kept_tiles, SMEM), (branch, SMEM)]
        + [(a, VMEM) for a in (left_own, left_one, right_own, left_two, right_next, earlier, density)],
        [jax.ShapeDtypeStruct((block_rows, size), jnp.bfloat16), jax.ShapeDtypeStruct((8, LANES), jnp.float32)],
        [HBM, VMEM],
        [pltpu.VMEM((block_rows, size), kind), pltpu.SemaphoreType.DMA((8,))],
    )

    occupation = call(
        functools.partial(total_kernel, row_count * block_rows),
        "total",
        [(parts, VMEM), (stored, VMEM)],
        jax.ShapeDtypeStruct((1,), jnp.float32),
        SMEM,
    )
    return new_density, occupation


def solution(mesh):
    mesh = jax.sharding.Mesh(mesh.devices.reshape(SIZES), AXES)
    whole = P(ROW, COL)
    in_specs = (whole,) * 7 + (P(ROW),)
    return jax.shard_map(local, mesh=mesh, in_specs=in_specs, out_specs=(whole, P()), check_vma=False)
```

```python
import functools

import jax
import jax.numpy as jnp
from jax import lax
from jax.experimental import pallas as pl
from jax.experimental.pallas import tpu as pltpu
from jax.sharding import PartitionSpec as P

FLAG_ROWS = 16
LANES = 128

VMEM = pl.BlockSpec(memory_space=pltpu.VMEM)
SMEM = pl.BlockSpec(memory_space=pltpu.SMEM)
HBM = pl.BlockSpec(memory_space=pltpu.HBM)


def call(kernel, name, ins, outs, out_specs, scratch=(), limit=12 * 2**20):
    return pl.pallas_call(
        kernel,
        out_shape=outs,
        in_specs=[spec for _, spec in ins],
        out_specs=out_specs,
        scratch_shapes=list(scratch),
        compiler_params=pltpu.CompilerParams(vmem_limit_bytes=limit),
        name=name,
    )(*[array for array, _ in ins])


def shift(value, axis, steps):
    count = lax.axis_size(axis)
    return lax.ppermute(value, axis, [(src, (src + steps) % count) for src in range(count)])


def pack_kernel(*refs):
    occupied, panels, packed, (stage, flags, in_sems, out_sems, flag_sems) = refs[:2], refs[2:4], refs[4:6], refs[6:]
    size = stage.shape[3]
    asked = [pltpu.make_async_copy(occupied[side], flags.at[side], flag_sems.at[side]) for side in range(2)]
    loads = [
        pltpu.make_async_copy(panels[side].at[pl.ds(half * size, size)], stage.at[side, half, :size], in_sems.at[side, half])
        for side in range(2)
        for half in range(2)
    ]
    for copy in asked + loads:
        copy.start()
    for side in range(2):
        asked[side].wait()
        lanes = lax.broadcasted_iota(jnp.int32, (FLAG_ROWS, size), 1)
        values = [flags[side, k].astype(jnp.float32) for k in range(2)]
        rows = jnp.where(lanes < size // 2, values[0], values[1]).astype(stage.dtype)
        for half in range(2):
            stage[side, half, size:, :] = rows
    for copy in loads:
        copy.wait()
    stores = [
        pltpu.make_async_copy(stage.at[side, flags[side, 1]], packed[side], out_sems.at[side]) for side in range(2)
    ]
    for store in stores:
        store.start()
    for store in stores:
        store.wait()


def base_kernel(right_occupied, kept, branch, right_own, earlier, density, base, wanted, right_here, earlier_tile, density_tile, sems):
    size = earlier_tile.shape[0]
    row, col = lax.axis_index(ROW), lax.axis_index(COL)
    half = lax.rem(col, 2)
    base[...] = jnp.zeros_like(base)
    wanted[...] = jnp.full(wanted.shape, right_occupied[1], wanted.dtype)
    right_here[...] = right_own[...]

    @pl.when(lax.div(col, 2) == row)
    def _mine():
        rows = pl.ds(pl.multiple_of(half * size, size), size)
        copies = [
            pltpu.make_async_copy(earlier.at[rows], earlier_tile, sems.at[0]),
            pltpu.make_async_copy(density.at[rows], density_tile, sems.at[1]),
        ]
        for copy in copies:
            copy.start()
        for copy in copies:
            copy.wait()
        once = jnp.zeros((1, 1), jnp.float32)
        twice = jnp.zeros((1, 1), jnp.float32)
        for start in range(0, size, LANES):
            part = pl.ds(start, LANES)
            once = once + diagonal(earlier_tile[part, part].astype(jnp.float32))
            twice = twice + diagonal(2.0 * density_tile[part, part].astype(jnp.float32))
        squared = branch[half] == 1
        keep = (kept[half] == 1).astype(jnp.float32)
        lanes = lax.broadcasted_iota(jnp.int32, base.shape, 1)
        value = keep * jnp.where(squared, once, twice - once)
        weight = jnp.where(squared, keep, -keep)
        high = lax.axis_index("x_hi")
        base[...] = jnp.where(lanes == 0, value, 0.0) + jnp.where(lanes == 3 + high, weight, 0.0)


def flag_pair(payload):
    size = payload.shape[1]
    tail = payload[size:, :].astype(jnp.float32)
    return tail[0:1, 0:1], tail[0:1, size // 2 : size // 2 + 1]


def dot(a, b):
    return jnp.dot(a, b, preferred_element_type=jnp.float32)


def diagonal(block):
    rows = lax.broadcasted_iota(jnp.int32, block.shape, 0)
    cols = lax.broadcasted_iota(jnp.int32, block.shape, 1)
    return jnp.sum(jnp.where(rows == cols, block, 0.0), axis=(0, 1), keepdims=True)


def product_trace(left, right, size):
    total = jnp.zeros((1, 1), jnp.float32)
    for start in range(0, size, LANES):
        part = pl.ds(start, LANES)
        total = total + diagonal(dot(left(part), right[:size, part]))
    return total


def far_here():
    row, col = lax.axis_index(ROW), lax.axis_index(COL)
    count = lax.axis_size(COL)
    return lax.div(lax.rem(col + count - 2, count), 2) == row


def decide_kernel(wanted, right_trace, second):
    second[...] = wanted[...]

    @pl.when(far_here())
    def _far():
        flag = flag_pair(right_trace)[1].astype(second.dtype)
        second[...] = jnp.broadcast_to(flag, second.shape)


def choose_kernel(second, own, one, parts, chosen):
    use_one = jnp.max(second[...]) == 1

    @pl.when(use_one)
    def _one():
        chosen[...] = one[...]

    @pl.when(jnp.logical_not(use_one))
    def _own():
        chosen[...] = own[...]


def trace_kernel(own, one, right_own, right_trace, base, parts):
    size = own.shape[1]
    row, col = lax.axis_index(ROW), lax.axis_index(COL)
    half = lax.rem(col, 2)
    lanes = lax.broadcasted_iota(jnp.int32, (1, LANES), 1)
    parts[...] = jnp.zeros_like(parts)

    @pl.when(lax.div(col, 2) == row)
    def _near():
        right_flags = flag_pair(right_own)
        second = jnp.max(right_flags[1]) == 1.0
        value = product_trace(lambda part: jnp.where(second, one[part, :], own[part, :]), right_own, size)
        flags = [jnp.where(second, a, b) for a, b in zip(flag_pair(one), flag_pair(own))]
        value = value * jnp.where(half == 1, flags[1], flags[0]) * (right_flags[0] + right_flags[1])
        known = base[0:1, :]
        weight = jnp.sum(jnp.where(lanes == 3 + lax.axis_index("x_hi"), known, 0.0), axis=1, keepdims=True)
        parts[...] += known + jnp.where(lanes == 0, value * weight, 0.0)

    @pl.when(far_here())
    def _far():
        right_flags = flag_pair(right_trace)
        second = jnp.max(right_flags[1]) == 1.0
        value = product_trace(lambda part: jnp.where(second, one[part, :], own[part, :]), right_trace, size)
        flags = [jnp.where(second, a, b) for a, b in zip(flag_pair(one), flag_pair(own))]
        value = value * jnp.where(half == 1, flags[1], flags[0]) * (right_flags[0] + right_flags[1])
        parts[...] += jnp.where(lanes == 1 + lax.axis_index("x_hi"), value, 0.0)


def middle_kernel(parts, spread):
    spread[...] = jnp.broadcast_to(jnp.sum(parts[...], axis=0, keepdims=True), spread.shape)


def total_kernel(order, parts, stored, occupation):
    values = parts[...]
    lanes = lax.broadcasted_iota(jnp.int32, values.shape, 1)
    planes = lax.broadcasted_iota(jnp.int32, (values.shape[0], 1), 0)
    moved = jnp.concatenate([values[-2:], values[:-2]], axis=0)

    def lane(array, index):
        return jnp.sum(jnp.where(lanes == index, array, 0.0), axis=1, keepdims=True)

    low, high = lane(moved, 3), lane(moved, 4)
    low, high = jnp.where(planes < 2, high, low), jnp.where(planes < 2, low, high)
    occupation[0] = jnp.sum(lane(values, 0) + lane(values, 1) * low + lane(values, 2) * high) / order


def last_kernel(
    right_occupied, kept, branch, own, one, right_own, two, right_next, earlier, density, out, stored, result, sems
):
    size = own.shape[1]
    step = size // 4
    stored[...] = jnp.zeros_like(stored)
    second = right_occupied[1] == 1
    occupied = (right_occupied[0] + right_occupied[1]).astype(jnp.float32)
    first_flags = [jnp.where(second, a, b) * occupied for a, b in zip(flag_pair(one), flag_pair(own))]
    right_flags = flag_pair(right_next)
    last_flags = [flag * (right_flags[0] + right_flags[1]) for flag in flag_pair(two)]
    signs = [jnp.where(branch[half] == 1, 1.0, -1.0) for half in range(2)]
    stores = []
    for start in range(0, size, step):
        part = pl.ds(start, step)
        first = dot(jnp.where(second, one[part, :], own[part, :]), right_own[:size, :])
        last = dot(two[part, :], right_next[:size, :])
        for half in range(2):
            rows = pl.ds(half * size + start, step)
            product = earlier[rows, :].astype(jnp.float32) + first_flags[half] * first + last_flags[half] * last
            value = signs[half] * product + (1.0 - signs[half]) * density[rows, :].astype(jnp.float32)
            value = jnp.where(kept[half] == 1, value, 0.0)
            result[rows, :] = value.astype(result.dtype)
            store = pltpu.make_async_copy(result.at[rows], out.at[rows], sems.at[len(stores)])
            store.start()
            stores.append(store)
    for store in stores:
        store.wait()


def spread_over(rows, axis):
    return lax.all_to_all(rows, axis, 0, 0, tiled=True)


AXES = ("y", "x_lo", "core", "x_hi", "z")
SIZES = (4, 2, 2, 2, 16)
ROW, COL, PLANE = AXES[:3], AXES[3:], AXES[:4]


def local(left_panel, right_panel, earlier, density, left_occupied, right_occupied, kept_tiles, branch):
    block_rows, size = left_panel.shape
    row_count, col_count = lax.axis_size(ROW), lax.axis_size(COL)
    both = AXES
    left_occupied, right_occupied, kept_tiles = (a.reshape(2) for a in (left_occupied, right_occupied, kept_tiles))
    kind = left_panel.dtype
    payload = jax.ShapeDtypeStruct((size + FLAG_ROWS, size), kind)

    left_own, right_own = call(
        pack_kernel,
        "pack",
        [(left_occupied, HBM), (right_occupied, HBM), (left_panel, HBM), (right_panel, HBM)],
        [payload, payload],
        [HBM, HBM],
        [
            pltpu.VMEM((2, 2) + payload.shape, kind),
            pltpu.SMEM((2, 2), jnp.int32),
            pltpu.SemaphoreType.DMA((2, 2)),
            pltpu.SemaphoreType.DMA((2,)),
            pltpu.SemaphoreType.DMA((2,)),
        ],
        62 * 2**20,
    )
    left_one = shift(left_own, COL, -1)

    to_trace = [
        (((j // 2 + 1) % row_count) * col_count + j, (j // 2) * col_count + (j + 2) % col_count)
        for j in range(col_count)
    ]
    right_trace = lax.ppermute(right_own, both, to_trace)

    base, wanted, right_here = call(
        base_kernel,
        "base",
        [(right_occupied, SMEM), (kept_tiles, SMEM), (branch, SMEM), (right_own, VMEM), (earlier, HBM), (density, HBM)],
        [jax.ShapeDtypeStruct((8, LANES), jnp.float32), jax.ShapeDtypeStruct((8, LANES), jnp.int32), payload],
        [VMEM, VMEM, VMEM],
        [pltpu.VMEM((size, size), kind), pltpu.VMEM((size, size), kind), pltpu.SemaphoreType.DMA((2,))],
    )

    to_wanted = [
        (((i + 1) % row_count) * col_count + j, i * col_count + (j + 2) % col_count)
        for i in range(row_count)
        for j in range(col_count)
        if j // 2 != i
    ]
    wanted = lax.ppermute(wanted, both, to_wanted)
    right_next = shift(right_own, ROW, -1)

    second = call(
        decide_kernel,
        "decide",
        [(wanted, VMEM), (right_trace, VMEM)],
        jax.ShapeDtypeStruct((8, LANES), jnp.int32),
        VMEM,
    )
    parts = call(
        trace_kernel,
        "trace",
        [(a, VMEM) for a in (left_own, left_one, right_here, right_trace, base)],
        jax.ShapeDtypeStruct((lax.axis_size(PLANE), LANES), jnp.float32),
        VMEM,
    )

    chosen = call(choose_kernel, "choose", [(a, VMEM) for a in (second, left_own, left_one, parts)], payload, VMEM)
    left_two = shift(chosen, COL, -2)
    parts = spread_over(parts, PLANE)
    parts = call(
        middle_kernel, "middle", [(parts, VMEM)], jax.ShapeDtypeStruct((lax.axis_size("z"), LANES), jnp.float32), VMEM
    )
    parts = spread_over(parts, "z")
    new_density, stored = call(
        last_kernel,
        "last",
        [(right_occupied, SMEM), (kept_tiles, SMEM), (branch, SMEM)]
        + [(a, VMEM) for a in (left_own, left_one, right_own, left_two, right_next, earlier, density)],
        [jax.ShapeDtypeStruct((block_rows, size), jnp.bfloat16), jax.ShapeDtypeStruct((8, LANES), jnp.float32)],
        [HBM, VMEM],
        [pltpu.VMEM((block_rows, size), kind), pltpu.SemaphoreType.DMA((8,))],
    )

    occupation = call(
        functools.partial(total_kernel, row_count * block_rows),
        "total",
        [(parts, VMEM), (stored, VMEM)],
        jax.ShapeDtypeStruct((1,), jnp.float32),
        SMEM,
    )
    return new_density, occupation


def solution(mesh):
    mesh = jax.sharding.Mesh(mesh.devices.reshape(SIZES), AXES)
    whole = P(ROW, COL)
    in_specs = (whole,) * 7 + (P(ROW),)
    return jax.shard_map(local, mesh=mesh, in_specs=in_specs, out_specs=(whole, P()), check_vma=False)
```

```python
import functools

import jax
import jax.numpy as jnp
from jax import lax
from jax.experimental import pallas as pl
from jax.experimental.pallas import tpu as pltpu
from jax.sharding import PartitionSpec as P

FLAG_ROWS = 16
LANES = 128

VMEM = pl.BlockSpec(memory_space=pltpu.VMEM)
SMEM = pl.BlockSpec(memory_space=pltpu.SMEM)
HBM = pl.BlockSpec(memory_space=pltpu.HBM)


def call(kernel, name, ins, outs, out_specs, scratch=(), limit=12 * 2**20):
    return pl.pallas_call(
        kernel,
        out_shape=outs,
        in_specs=[spec for _, spec in ins],
        out_specs=out_specs,
        scratch_shapes=list(scratch),
        compiler_params=pltpu.CompilerParams(vmem_limit_bytes=limit),
        name=name,
    )(*[array for array, _ in ins])


def shift(value, axis, steps):
    count = lax.axis_size(axis)
    return lax.ppermute(value, axis, [(src, (src + steps) % count) for src in range(count)])


def pack_kernel(*refs):
    occupied, panels, packed, (stage, flags, in_sems, out_sems, flag_sems) = refs[:2], refs[2:4], refs[4:6], refs[6:]
    size = stage.shape[3]
    asked = [pltpu.make_async_copy(occupied[side], flags.at[side], flag_sems.at[side]) for side in range(2)]
    loads = [
        pltpu.make_async_copy(panels[side].at[pl.ds(half * size, size)], stage.at[side, half, :size], in_sems.at[side, half])
        for side in range(2)
        for half in range(2)
    ]
    for copy in asked + loads:
        copy.start()
    for side in range(2):
        asked[side].wait()
        lanes = lax.broadcasted_iota(jnp.int32, (FLAG_ROWS, size), 1)
        values = [flags[side, k].astype(jnp.float32) for k in range(2)]
        rows = jnp.where(lanes < size // 2, values[0], values[1]).astype(stage.dtype)
        for half in range(2):
            stage[side, half, size:, :] = rows
    for copy in loads:
        copy.wait()
    stores = [
        pltpu.make_async_copy(stage.at[side, flags[side, 1]], packed[side], out_sems.at[side]) for side in range(2)
    ]
    for store in stores:
        store.start()
    for store in stores:
        store.wait()


def wanted_kernel(right_occupied, wanted):
    wanted[...] = jnp.full(wanted.shape, right_occupied[1], wanted.dtype)


def copy_kernel(after, source, copied):
    copied[...] = source[...]


def base_kernel(kept, branch, right_own, earlier, density, base, right_here, earlier_tile, density_tile, sems):
    size = earlier_tile.shape[0]
    row, col = lax.axis_index(ROW), lax.axis_index(COL)
    half = lax.rem(col, 2)
    base[...] = jnp.zeros_like(base)
    right_here[...] = right_own[...]

    @pl.when(lax.div(col, 2) == row)
    def _mine():
        rows = pl.ds(pl.multiple_of(half * size, size), size)
        copies = [
            pltpu.make_async_copy(earlier.at[rows], earlier_tile, sems.at[0]),
            pltpu.make_async_copy(density.at[rows], density_tile, sems.at[1]),
        ]
        for copy in copies:
            copy.start()
        for copy in copies:
            copy.wait()
        once = jnp.zeros((1, 1), jnp.float32)
        twice = jnp.zeros((1, 1), jnp.float32)
        for start in range(0, size, LANES):
            part = pl.ds(start, LANES)
            once = once + diagonal(earlier_tile[part, part].astype(jnp.float32))
            twice = twice + diagonal(2.0 * density_tile[part, part].astype(jnp.float32))
        squared = branch[half] == 1
        keep = (kept[half] == 1).astype(jnp.float32)
        lanes = lax.broadcasted_iota(jnp.int32, base.shape, 1)
        value = keep * jnp.where(squared, once, twice - once)
        weight = jnp.where(squared, keep, -keep)
        high = lax.axis_index("x_hi")
        base[...] = jnp.where(lanes == 0, value, 0.0) + jnp.where(lanes == 3 + high, weight, 0.0)


def flag_pair(payload):
    size = payload.shape[1]
    tail = payload[size:, :].astype(jnp.float32)
    return tail[0:1, 0:1], tail[0:1, size // 2 : size // 2 + 1]


def dot(a, b):
    return jnp.dot(a, b, preferred_element_type=jnp.float32)


def diagonal(block):
    rows = lax.broadcasted_iota(jnp.int32, block.shape, 0)
    cols = lax.broadcasted_iota(jnp.int32, block.shape, 1)
    return jnp.sum(jnp.where(rows == cols, block, 0.0), axis=(0, 1), keepdims=True)


def product_trace(left, right, size):
    total = jnp.zeros((1, 1), jnp.float32)
    for start in range(0, size, LANES):
        part = pl.ds(start, LANES)
        total = total + diagonal(dot(left(part), right[:size, part]))
    return total


def far_here():
    row, col = lax.axis_index(ROW), lax.axis_index(COL)
    count = lax.axis_size(COL)
    return lax.div(lax.rem(col + count - 2, count), 2) == row


def decide_kernel(wanted, right_trace, second):
    second[...] = wanted[...]

    @pl.when(far_here())
    def _far():
        flag = flag_pair(right_trace)[1].astype(second.dtype)
        second[...] = jnp.broadcast_to(flag, second.shape)


def choose_kernel(second, own, one, parts, chosen):
    use_one = jnp.max(second[...]) == 1

    @pl.when(use_one)
    def _one():
        chosen[...] = one[...]

    @pl.when(jnp.logical_not(use_one))
    def _own():
        chosen[...] = own[...]


def trace_kernel(own, one, right_own, right_trace, base, parts):
    size = own.shape[1]
    row, col = lax.axis_index(ROW), lax.axis_index(COL)
    half = lax.rem(col, 2)
    lanes = lax.broadcasted_iota(jnp.int32, (1, LANES), 1)
    parts[...] = jnp.zeros_like(parts)

    @pl.when(lax.div(col, 2) == row)
    def _near():
        right_flags = flag_pair(right_own)
        second = jnp.max(right_flags[1]) == 1.0
        value = product_trace(lambda part: jnp.where(second, one[part, :], own[part, :]), right_own, size)
        flags = [jnp.where(second, a, b) for a, b in zip(flag_pair(one), flag_pair(own))]
        value = value * jnp.where(half == 1, flags[1], flags[0]) * (right_flags[0] + right_flags[1])
        known = base[0:1, :]
        weight = jnp.sum(jnp.where(lanes == 3 + lax.axis_index("x_hi"), known, 0.0), axis=1, keepdims=True)
        parts[...] += known + jnp.where(lanes == 0, value * weight, 0.0)

    @pl.when(far_here())
    def _far():
        right_flags = flag_pair(right_trace)
        second = jnp.max(right_flags[1]) == 1.0
        value = product_trace(lambda part: jnp.where(second, one[part, :], own[part, :]), right_trace, size)
        flags = [jnp.where(second, a, b) for a, b in zip(flag_pair(one), flag_pair(own))]
        value = value * jnp.where(half == 1, flags[1], flags[0]) * (right_flags[0] + right_flags[1])
        parts[...] += jnp.where(lanes == 1 + lax.axis_index("x_hi"), value, 0.0)


def middle_kernel(parts, spread):
    spread[...] = jnp.broadcast_to(jnp.sum(parts[...], axis=0, keepdims=True), spread.shape)


def total_kernel(order, parts, stored, occupation):
    values = parts[...]
    lanes = lax.broadcasted_iota(jnp.int32, values.shape, 1)
    planes = lax.broadcasted_iota(jnp.int32, (values.shape[0], 1), 0)
    moved = jnp.concatenate([values[-2:], values[:-2]], axis=0)

    def lane(array, index):
        return jnp.sum(jnp.where(lanes == index, array, 0.0), axis=1, keepdims=True)

    low, high = lane(moved, 3), lane(moved, 4)
    low, high = jnp.where(planes < 2, high, low), jnp.where(planes < 2, low, high)
    occupation[0] = jnp.sum(lane(values, 0) + lane(values, 1) * low + lane(values, 2) * high) / order


def last_kernel(
    right_occupied, kept, branch, own, one, right_own, two, right_next, earlier, density, out, stored, result, sems
):
    size = own.shape[1]
    step = size // 4
    stored[...] = jnp.zeros_like(stored)
    second = right_occupied[1] == 1
    occupied = (right_occupied[0] + right_occupied[1]).astype(jnp.float32)
    first_flags = [jnp.where(second, a, b) * occupied for a, b in zip(flag_pair(one), flag_pair(own))]
    right_flags = flag_pair(right_next)
    last_flags = [flag * (right_flags[0] + right_flags[1]) for flag in flag_pair(two)]
    signs = [jnp.where(branch[half] == 1, 1.0, -1.0) for half in range(2)]
    stores = []
    for start in range(0, size, step):
        part = pl.ds(start, step)
        first = dot(jnp.where(second, one[part, :], own[part, :]), right_own[:size, :])
        last = dot(two[part, :], right_next[:size, :])
        for half in range(2):
            rows = pl.ds(half * size + start, step)
            product = earlier[rows, :].astype(jnp.float32) + first_flags[half] * first + last_flags[half] * last
            value = signs[half] * product + (1.0 - signs[half]) * density[rows, :].astype(jnp.float32)
            value = jnp.where(kept[half] == 1, value, 0.0)
            result[rows, :] = value.astype(result.dtype)
            store = pltpu.make_async_copy(result.at[rows], out.at[rows], sems.at[len(stores)])
            store.start()
            stores.append(store)
    for store in stores:
        store.wait()


def spread_over(rows, axis):
    return lax.all_to_all(rows, axis, 0, 0, tiled=True)


AXES = ("y", "x_lo", "core", "x_hi", "z")
SIZES = (4, 2, 2, 2, 16)
ROW, COL, PLANE = AXES[:3], AXES[3:], AXES[:4]


def local(left_panel, right_panel, earlier, density, left_occupied, right_occupied, kept_tiles, branch):
    block_rows, size = left_panel.shape
    row_count, col_count = lax.axis_size(ROW), lax.axis_size(COL)
    both = AXES
    left_occupied, right_occupied, kept_tiles = (a.reshape(2) for a in (left_occupied, right_occupied, kept_tiles))
    kind = left_panel.dtype
    payload = jax.ShapeDtypeStruct((size + FLAG_ROWS, size), kind)

    left_own, right_own = call(
        pack_kernel,
        "pack",
        [(left_occupied, HBM), (right_occupied, HBM), (left_panel, HBM), (right_panel, HBM)],
        [payload, payload],
        [HBM, HBM],
        [
            pltpu.VMEM((2, 2) + payload.shape, kind),
            pltpu.SMEM((2, 2), jnp.int32),
            pltpu.SemaphoreType.DMA((2, 2)),
            pltpu.SemaphoreType.DMA((2,)),
            pltpu.SemaphoreType.DMA((2,)),
        ],
        62 * 2**20,
    )
    left_one = shift(left_own, COL, -1)

    to_trace = [
        (((j // 2 + 1) % row_count) * col_count + j, (j // 2) * col_count + (j + 2) % col_count)
        for j in range(col_count)
    ]
    right_trace = lax.ppermute(right_own, both, to_trace)

    base, right_here = call(
        base_kernel,
        "base",
        [(kept_tiles, SMEM), (branch, SMEM), (right_own, VMEM), (earlier, HBM), (density, HBM)],
        [jax.ShapeDtypeStruct((8, LANES), jnp.float32), payload],
        [VMEM, VMEM],
        [pltpu.VMEM((size, size), kind), pltpu.VMEM((size, size), kind), pltpu.SemaphoreType.DMA((2,))],
    )

    to_wanted = [
        (((i + 1) % row_count) * col_count + j, i * col_count + (j + 2) % col_count)
        for i in range(row_count)
        for j in range(col_count)
        if j // 2 != i
    ]
    wanted = call(
        wanted_kernel, "wanted", [(right_occupied, SMEM)], jax.ShapeDtypeStruct((8, LANES), jnp.int32), VMEM
    )
    wanted = lax.ppermute(wanted, both, to_wanted)

    right_sent = call(copy_kernel, "sent", [(wanted, VMEM), (right_own, VMEM)], payload, VMEM)
    right_next = shift(right_sent, ROW, -1)
    second = call(
        decide_kernel,
        "decide",
        [(wanted, VMEM), (right_trace, VMEM)],
        jax.ShapeDtypeStruct((8, LANES), jnp.int32),
        VMEM,
    )
    parts = call(
        trace_kernel,
        "trace",
        [(a, VMEM) for a in (left_own, left_one, right_here, right_trace, base)],
        jax.ShapeDtypeStruct((lax.axis_size(PLANE), LANES), jnp.float32),
        VMEM,
    )

    chosen = call(choose_kernel, "choose", [(a, VMEM) for a in (second, left_own, left_one, parts)], payload, VMEM)
    left_two = shift(chosen, COL, -2)
    parts = spread_over(parts, PLANE)
    parts = call(
        middle_kernel, "middle", [(parts, VMEM)], jax.ShapeDtypeStruct((lax.axis_size("z"), LANES), jnp.float32), VMEM
    )
    parts = spread_over(parts, "z")
    new_density, stored = call(
        last_kernel,
        "last",
        [(right_occupied, SMEM), (kept_tiles, SMEM), (branch, SMEM)]
        + [(a, VMEM) for a in (left_own, left_one, right_own, left_two, right_next, earlier, density)],
        [jax.ShapeDtypeStruct((block_rows, size), jnp.bfloat16), jax.ShapeDtypeStruct((8, LANES), jnp.float32)],
        [HBM, VMEM],
        [pltpu.VMEM((block_rows, size), kind), pltpu.SemaphoreType.DMA((8,))],
    )

    occupation = call(
        functools.partial(total_kernel, row_count * block_rows),
        "total",
        [(parts, VMEM), (stored, VMEM)],
        jax.ShapeDtypeStruct((1,), jnp.float32),
        SMEM,
    )
    return new_density, occupation


def solution(mesh):
    mesh = jax.sharding.Mesh(mesh.devices.reshape(SIZES), AXES)
    whole = P(ROW, COL)
    in_specs = (whole,) * 7 + (P(ROW),)
    return jax.shard_map(local, mesh=mesh, in_specs=in_specs, out_specs=(whole, P()), check_vma=False)
```
